32 devices in a mesh: groups: 2 (over x), tm: 8 (over z, y), row: 2 (over core).
Axes of the slice: x: 2, y: 2, z: 4, core: 2. Of those that a mesh axis runs over, the one named last changes fastest.
Arguments:
- latent: bfloat16 [64, 4, 64, 384], P(('groups', 'tm'), 'row'), parts along dimension 0, may hold values from -6 to 6
- conv_gain: bfloat16 [384], replicated, may hold values from 0.099609375 to 1.8984375
- conv_weight: bfloat16 [3, 3, 3, 384, 384], replicated, may hold values from -0.0625 to 0.0625
- conv_bias: bfloat16 [384], replicated, may hold values from -3 to 3
- attn_gain: bfloat16 [384], replicated, may hold values from 0.099609375 to 1.8984375
- w_query: bfloat16 [384, 384], replicated, may hold values from -1.5309311 to 1.5309311
- w_key: bfloat16 [384, 384], replicated, may hold values from -1.5309311 to 1.5309311
- w_value: bfloat16 [384, 384], replicated, may hold values from -0.3125 to 0.3125
- w_out: bfloat16 [384, 384], replicated, may hold values from -0.3125 to 0.3125
- time_weight: bfloat16 [3, 384, 768], replicated, may hold values from -0.1875 to 0.1875
- time_bias: bfloat16 [768], replicated, may hold values from -3 to 3
Outputs:
- upsampled: bfloat16 [128, 4, 64, 384], P(('groups', 'tm'), 'row'), parts along dimension 0
The draws below stay inside these ranges and needn't reach their ends.
There are 2 independent parts, one for each index of `groups`. The reference program is written for one: setup_inputs(seed, part) draws one part's arguments, and reference() takes and returns one part's arrays. A program takes and returns all parts, laid end to end along the dimension named above; an argument that names none is the same for every part. Nothing has to cross between parts.
All inputs are finite; a program needn't handle non-finite values.
Results may differ from the reference program's by a relative error of at most 0.017.
Values may be sent and summed in bfloat16 or wider, within the bound.
A program may use at most 64 MiB of HBM per device.

```python
import jax
import jax.numpy as jnp
from jax import lax

C = 384
COLS = 64
FRAMES = 32
ROWS = 4


def draw_w_key(key, part):
    own = jax.random.truncated_normal(jax.random.fold_in(key, 12), -4.0, 4.0, (C, C), jnp.float32)
    matrix = own
    return (matrix * C ** (-0.5)).astype(jnp.bfloat16)


def draw_w_query(key, part):
    own = jax.random.truncated_normal(jax.random.fold_in(key, 13), -4.0, 4.0, (C, C), jnp.float32)
    matrix = own
    return (matrix * C ** (-0.5)).astype(jnp.bfloat16)


def block_scale(own_key, dims, shards, smallest, top_value):
    loudness, own = 1.0, jax.random.fold_in(own_key, 6)
    for axis_at, shards_of in shards:
        steps = jnp.exp(jax.random.uniform(jax.random.fold_in(own, axis_at), (shards_of,), jnp.float32, smallest / len(shards), top_value / len(shards)))
        loudness = loudness * jnp.repeat(steps, dims[axis_at] // shards_of).reshape([-1 if axis == axis_at else 1 for axis in range(len(dims))])
    return loudness


def scatter_about(own_key, extent, spread, bound, cuts=(), held_as=jnp.bfloat16):
    result = spread * jax.random.normal(own_key, extent, jnp.float32)
    if cuts:
        result = result * block_scale(own_key, extent, cuts, -0.22, 0.18)
    return jnp.clip(result, -bound, bound).astype(held_as)


def setup_inputs(seed: int = 0, part: int = 0) -> dict:
    streams_of = jax.random.split(jax.random.key(seed), 12)
    own_keys = jax.random.split(jax.random.fold_in(streams_of[11], part), 12)
    return {
        "latent": scatter_about(own_keys[0], (FRAMES, ROWS, COLS, C), 1.0, 6.0, ((0, 8), (1, 2))),
        "conv_gain": jnp.clip(1.0 + 0.18 * jax.random.normal(streams_of[1], (C,), jnp.float32), 0.099609375, 1.8984375).astype(jnp.bfloat16),
        "conv_weight": scatter_about(streams_of[2], (3, 3, 3, C, C), (27 * C) ** -0.5, 0.0625),
        "conv_bias": scatter_about(streams_of[3], (C,), 0.5, 3.0),
        "attn_gain": jnp.clip(1.0 + 0.18 * jax.random.normal(streams_of[4], (C,), jnp.float32), 0.099609375, 1.8984375).astype(jnp.bfloat16),
        "w_query": draw_w_query(jax.random.fold_in(streams_of[11], 71), part),
        "w_key": draw_w_key(jax.random.fold_in(streams_of[11], 71), part),
        "w_value": scatter_about(streams_of[7], (C, C), C ** -0.5, 0.3125),
        "w_out": scatter_about(streams_of[8], (C, C), C ** -0.5, 0.3125),
        "time_weight": scatter_about(streams_of[9], (3, C, 2 * C), (3 * C) ** -0.5, 0.1875),
        "time_bias": scatter_about(streams_of[10], (2 * C,), 0.5, 3.0),
    }


def channel_norm(values, gain):
    floats = values.astype(jnp.float32)
    return floats * lax.rsqrt(lax.optimization_barrier(jnp.mean(floats * floats, axis=-1, keepdims=True)) + 1e-06) * gain.astype(jnp.float32)

def reference(latent, conv_gain, conv_weight, conv_bias, attn_gain, w_query, w_key, w_value, w_out, time_weight, time_bias):
    activated = jax.nn.silu(channel_norm(latent, conv_gain)).astype(jnp.bfloat16)
    padded = jnp.pad(activated.astype(jnp.float32), ((2, 0), (1, 1), (1, 1), (0, 0)))
    conved = lax.conv_general_dilated(padded[None], conv_weight.astype(jnp.float32), (1, 1, 1), 'VALID', dimension_numbers=('NDHWC', 'DHWIO', 'NDHWC'), precision=lax.Precision.HIGHEST)[0]
    hidden = (latent.astype(jnp.float32) + conved + conv_bias.astype(jnp.float32)).astype(jnp.bfloat16)
    attn_in = channel_norm(hidden, attn_gain).astype(jnp.bfloat16)
    flattened = attn_in.reshape(FRAMES * ROWS * COLS, C)

    def project(matrix):
        return jnp.dot(flattened, matrix, preferred_element_type=jnp.float32).astype(jnp.bfloat16).reshape(FRAMES, ROWS * COLS, C)
    query = project(w_query)
    keys = project(w_key)
    values = project(w_value)
    scores = jnp.einsum('tpc,spc->pts', query.astype(jnp.float32), keys.astype(jnp.float32)) * C ** (-0.5)
    later = lax.broadcasted_iota(jnp.int32, (FRAMES, FRAMES), 0)
    earlier = lax.broadcasted_iota(jnp.int32, (FRAMES, FRAMES), 1)
    causal_mask = (earlier <= later)[None]
    scores = jnp.where(causal_mask, scores, -1e+30)
    highest = lax.optimization_barrier(jnp.max(scores, axis=-1, keepdims=True))
    expo = jnp.where(causal_mask, jnp.exp(scores - highest), 0.0)
    weights = (expo / lax.optimization_barrier(jnp.sum(expo, axis=-1, keepdims=True))).astype(jnp.bfloat16)
    attended = jnp.einsum('pts,spc->tpc', weights.astype(jnp.float32), values.astype(jnp.float32)).astype(jnp.bfloat16)
    mixed_term = jnp.dot(attended.reshape(-1, C), w_out, preferred_element_type=jnp.float32).reshape(FRAMES, ROWS, COLS, C)
    mixed = (hidden.astype(jnp.float32) + mixed_term).astype(jnp.bfloat16)
    carried = jnp.pad(mixed, ((2, 0), (0, 0), (0, 0), (0, 0)))
    doubled = jnp.zeros((FRAMES * ROWS * COLS, 2 * C), jnp.float32) + time_bias.astype(jnp.float32)
    for offset in range(3):
        doubled = doubled + jnp.dot(carried[offset:offset + FRAMES].reshape(-1, C), time_weight[offset], preferred_element_type=jnp.float32)
    doubled = doubled.reshape(FRAMES, ROWS, COLS, 2, C).transpose(0, 3, 1, 2, 4)
    return doubled.reshape(2 * FRAMES, ROWS, COLS, C).astype(jnp.bfloat16)
```

```python
import functools

import jax
import jax.numpy as jnp
from jax import lax
from jax.experimental import pallas as pl
from jax.experimental.pallas import tpu as pltpu
from jax.sharding import PartitionSpec as P


def shifted(value, axis, steps):
    count = lax.axis_size(axis)
    leading, last = (max(0, -steps), min(count, count - steps))
    return lax.ppermute(value, axis, [(source, source + steps) for source in range(leading, last)])


def with_halo(block, sides, width):
    for axis, dim in sides:
        count = lax.axis_size(axis)
        forward = [(i, i + 1) for i in range(count - 1)]
        backward = [(target, source) for source, target in forward]
        low = lax.ppermute(
            lax.slice_in_dim(block, block.shape[dim] - width, None, axis=dim), axis, forward
        )
        high = lax.ppermute(lax.slice_in_dim(block, 0, width, axis=dim), axis, backward)
        block = jnp.concatenate([low, block, high], axis=dim)
    return block


def channel_norm(values, gain):
    floats = values.astype(jnp.float32)
    return (
        floats
        * lax.rsqrt(jnp.mean(floats * floats, axis=-1, keepdims=True) + 1e-06)
        * gain.astype(jnp.float32)
    )


def attend(query, keys, values):
    frame_count = query.shape[0]
    channels = query.shape[2]
    scores = jnp.einsum(
        "tnc,snc->nts", query, keys, preferred_element_type=jnp.float32
    ) * channels ** (-0.5)
    later = lax.broadcasted_iota(jnp.int32, (frame_count, frame_count), 0)
    earlier = lax.broadcasted_iota(jnp.int32, (frame_count, frame_count), 1)
    causal_mask = (earlier <= later)[None]
    scores = jnp.where(causal_mask, scores, -1e30)
    highest = jnp.max(scores, axis=-1, keepdims=True)
    expo = jnp.where(causal_mask, jnp.exp(scores - highest), 0.0)
    weights = (expo / jnp.sum(expo, axis=-1, keepdims=True)).astype(jnp.bfloat16)
    return jnp.einsum("nts,snc->tnc", weights, values, preferred_element_type=jnp.float32).astype(
        jnp.bfloat16
    )


def flatten_block(block):
    return block.reshape(block.shape[0], block.shape[2], block.shape[3])


def plain_body(
    latent,
    conv_gain,
    conv_weight,
    conv_bias,
    attn_gain,
    w_query,
    w_key,
    w_value,
    w_out,
    time_weight,
    time_bias,
):
    frame_count, row_count, col_count, channels = latent.shape
    peers = lax.axis_size("tm")
    activated = jax.nn.silu(channel_norm(latent, conv_gain)).astype(jnp.bfloat16)
    carried = shifted(activated[frame_count - 2 :], "tm", 1)
    extended = jnp.concatenate([carried, activated], axis=0)
    padded = with_halo(extended, (("row", 1),), 1)
    padded = jnp.pad(padded, ((0, 0), (0, 0), (1, 1), (0, 0)))
    summed = jnp.zeros((frame_count * row_count * col_count, channels), jnp.float32)
    for offset in range(3):
        patches = jnp.concatenate(
            [
                padded[
                    offset : offset + frame_count,
                    row_offset : row_offset + row_count,
                    col_offset : col_offset + col_count,
                ]
                for row_offset in range(3)
                for col_offset in range(3)
            ],
            axis=-1,
        )
        summed = summed + jnp.dot(
            patches.reshape(-1, 9 * channels),
            conv_weight[offset].reshape(9 * channels, channels),
            preferred_element_type=jnp.float32,
        )
    hidden = (
        latent.astype(jnp.float32) + summed.reshape(latent.shape) + conv_bias.astype(jnp.float32)
    ).astype(jnp.bfloat16)
    attn_in = channel_norm(hidden, attn_gain).astype(jnp.bfloat16)
    positions = row_count * col_count
    per_peer = positions // peers
    blocked = attn_in.reshape(frame_count, peers, per_peer, channels)
    flat = flatten_block(lax.all_to_all(blocked, "tm", split_axis=1, concat_axis=0, tiled=True))
    stacked = flat.reshape(-1, channels)

    def project(matrix):
        return (
            jnp.dot(stacked, matrix, preferred_element_type=jnp.float32)
            .astype(jnp.bfloat16)
            .reshape(flat.shape)
        )

    attended = attend(project(w_query), project(w_key), project(w_value))[:, None]
    returned = lax.all_to_all(attended, "tm", split_axis=0, concat_axis=1, tiled=True)
    mixed_term = jnp.dot(
        returned.reshape(-1, channels), w_out, preferred_element_type=jnp.float32
    ).reshape(latent.shape)
    mixed = (hidden.astype(jnp.float32) + mixed_term).astype(jnp.bfloat16)
    mixed_cache = shifted(mixed[frame_count - 2 :], "tm", 1)
    mixed_ext = jnp.concatenate([mixed_cache, mixed], axis=0)
    doubled = jnp.zeros(
        (frame_count * row_count * col_count, 2 * channels), jnp.float32
    ) + time_bias.astype(jnp.float32)
    for offset in range(3):
        doubled = doubled + jnp.dot(
            mixed_ext[offset : offset + frame_count].reshape(-1, channels),
            time_weight[offset],
            preferred_element_type=jnp.float32,
        )
    doubled = doubled.reshape(frame_count, row_count, col_count, 2, channels).transpose(
        0, 3, 1, 2, 4
    )
    return doubled.reshape(2 * frame_count, row_count, col_count, channels).astype(jnp.bfloat16)


BF16, F32 = jnp.bfloat16, jnp.float32
MESH = pl.DeviceIdType.MESH


def unit(floats):
    return floats * lax.rsqrt(jnp.mean(floats * floats, axis=-1, keepdims=True) + 1e-06)


def dot(left, right):
    return jnp.dot(left, right, preferred_element_type=F32)


def window_kernel(
    n,
    latent_hbm,
    cgain,
    cw_hbm,
    cbias,
    again,
    wq_hbm,
    wk_hbm,
    wv_hbm,
    wo_hbm,
    tw_hbm,
    tbias,
    out,
    lat,
    lhs,
    rowh,
    cw,
    acc,
    hid,
    wqkv,
    wo,
    tw,
    x,
    kbuf,
    vbuf,
    mbuf,
    mext,
    load_sem,
    cw_sem,
    halo_send,
    halo_recv,
    a_send,
    a_recv,
    b_send,
    b_recv,
):
    frames, rows, cols, chan = lat.shape
    per = rows * cols // n
    own = frames * per
    me = lax.axis_index("tm")
    row = lax.axis_index("row")
    other = 1 - row

    loads = [pltpu.make_async_copy(latent_hbm, lat, load_sem.at[0])]
    for i, w in enumerate((wq_hbm, wk_hbm, wv_hbm)):
        loads.append(
            pltpu.make_async_copy(w, wqkv.at[:, pl.ds(i * chan, chan)], load_sem.at[1 + i])
        )
    loads.append(pltpu.make_async_copy(wo_hbm, wo, load_sem.at[4]))
    loads.append(pltpu.make_async_copy(tw_hbm, tw, load_sem.at[5]))
    cw_loads = {
        (a, b, e): pltpu.make_async_copy(
            cw_hbm.at[a, b, e],
            cw.at[a, pl.ds(b * chan, chan), pl.ds(e * chan, chan)],
            cw_sem.at[a, 3 * b + e],
        )
        for a in (2, 1, 0)
        for b in range(3)
        for e in range(3)
    }
    loads[0].start()
    for c in cw_loads.values():
        c.start()
    for c in loads[1:]:
        c.start()

    barrier = pltpu.get_barrier_semaphore()
    for k in range(1, n):
        pl.semaphore_signal(
            barrier, inc=1, device_id={"tm": lax.rem(me + k, n)}, device_id_type=MESH
        )
    pl.semaphore_signal(barrier, inc=1, device_id={"row": other}, device_id_type=MESH)

    loads[0].wait()
    gain = cgain[...].astype(F32).reshape(1, 1, 1, chan)
    normed = unit(lat[...].astype(F32)) * gain
    act = (normed / (1.0 + jnp.exp(-normed))).astype(BF16)
    mid = pl.ds(chan, chan)
    lhs[2:, :, :, chan : 2 * chan] = act

    pl.semaphore_wait(barrier, n)

    to_next = pltpu.make_async_remote_copy(
        lhs.at[pl.ds(frames, 2), :, :, mid],
        lhs.at[pl.ds(0, 2), :, :, mid],
        halo_send.at[0],
        halo_recv.at[0],
        device_id={"tm": jnp.minimum(me + 1, n - 1)},
        device_id_type=MESH,
    )
    to_row = pltpu.make_async_remote_copy(
        lhs.at[pl.ds(2, frames), other, :, mid],
        rowh.at[pl.ds(2, frames)],
        halo_send.at[1],
        halo_recv.at[1],
        device_id={"row": other},
        device_id_type=MESH,
    )
    relay = pltpu.make_async_remote_copy(
        lhs.at[pl.ds(0, 2), other, :, mid],
        rowh.at[pl.ds(0, 2)],
        halo_send.at[2],
        halo_recv.at[2],
        device_id={"row": other},
        device_id_type=MESH,
    )

    @pl.when(me < n - 1)
    def _():
        to_next.start()

    to_row.start()

    def spread(lo, hi):
        lhs[lo:hi, 1, :, 0:chan] = lhs[lo:hi, 0, :, chan : 2 * chan]
        lhs[lo:hi, 0, :, 2 * chan :] = lhs[lo:hi, 1, :, chan : 2 * chan]

    def edges(lo, hi):
        edge = rowh[lo:hi]
        lhs[lo:hi, 0, :, 0:chan] = jnp.where(row == 1, edge, jnp.zeros_like(edge))
        lhs[lo:hi, 1, :, 2 * chan :] = jnp.where(row == 0, edge, jnp.zeros_like(edge))

    spread(2, frames + 2)
    to_row.wait_recv()
    edges(2, frames + 2)

    def taps(lo, hi, a):
        part = lhs[lo:hi].reshape((hi - lo) * rows * cols, 3 * chan)
        return dot(part, cw[a]).reshape(hi - lo, rows, cols, 3 * chan)

    def loaded(a):
        for b in range(3):
            for e in range(3):
                cw_loads[a, b, e].wait()

    loaded(2)
    acc[...] = taps(2, frames + 2, 2)
    loaded(1)
    acc[1:] += taps(2, frames + 1, 1)
    loaded(0)
    acc[2:] += taps(2, frames, 0)

    bias = cbias[...].astype(F32).reshape(1, chan)

    def finish(lo, hi):
        m = (hi - lo) * rows * cols
        y = acc[lo:hi].reshape(m, 3 * chan)
        col = lax.rem(lax.broadcasted_iota(jnp.int32, (m, chan), 0), cols)
        left = jnp.where(col == 0, 0.0, pltpu.roll(y[:, :chan], 1, 0))
        right = jnp.where(col == cols - 1, 0.0, pltpu.roll(y[:, 2 * chan :], m - 1, 0))
        total = left + y[:, chan : 2 * chan] + right
        value = lat[lo:hi].astype(F32).reshape(m, chan) + total + bias
        hid[lo:hi] = value.astype(BF16).reshape(hi - lo, rows, cols, chan)

    def place(p):
        return p * per // cols, pl.ds(p * per % cols, per)

    def scatter_copies(half, p):
        lo, count = (2, frames - 2) if half == 0 else (0, 2)
        r, c = place(p)
        source = hid.at[pl.ds(lo, count), r, c]
        target = x.at[pl.ds(frames * me + lo, count)]
        remote = pltpu.make_async_remote_copy(
            source,
            target,
            a_send.at[half, p],
            a_recv.at[half, me],
            device_id={"tm": p},
            device_id_type=MESH,
        )
        local = pltpu.make_async_copy(source, target, a_recv.at[half, me])
        return remote, local

    def start_to(copies, p):
        remote, local = copies

        @pl.when(p != me)
        def _():
            remote.start()

        @pl.when(p == me)
        def _():
            local.start()

    def send_done(copies, p):
        remote = copies[0]

        @pl.when(p != me)
        def _():
            remote.wait_send()

    finish(2, frames)
    for p in range(n):
        start_to(scatter_copies(0, p), p)

    @pl.when(me > 0)
    def _():
        to_next.wait_recv()
        relay.start()

    @pl.when(me == 0)
    def _():
        lhs[0:2, :, :, chan : 2 * chan] = jnp.zeros((2, rows, cols, chan), BF16)
        rowh[0:2] = jnp.zeros((2, cols, chan), BF16)

    spread(0, 2)

    @pl.when(me > 0)
    def _():
        relay.wait_recv()

    edges(0, 2)
    acc[0:1] += taps(1, 2, 1)
    acc[0:2] += taps(0, 2, 0)
    finish(0, 2)
    for p in range(n):
        start_to(scatter_copies(1, p), p)

    for c in loads[1:]:
        c.wait()
    mbuf[0:2] = jnp.zeros((2, per, chan), BF16)
    gain2 = again[...].astype(F32).reshape(1, chan)

    def return_copies(p):
        r, c = place(0)
        first = me * per
        source = mbuf.at[pl.ds(frames * p, frames + 2)]
        target = mext.at[:, first // cols, pl.ds(pl.multiple_of(lax.rem(first, cols), per), per)]
        remote = pltpu.make_async_remote_copy(
            source,
            target,
            b_send.at[p],
            b_recv.at[me],
            device_id={"tm": p},
            device_id_type=MESH,
        )
        return remote, pltpu.make_async_copy(source, target, b_recv.at[me])

    group = 2 if n % 2 == 0 else 1
    m = group * own
    for j in range(n // group):
        for p in range(j * group, (j + 1) * group):
            for half, (lo, count) in enumerate(((2, frames - 2), (0, 2))):
                landed = x.at[pl.ds(frames * p + lo, count)]
                pltpu.make_async_copy(landed, landed, a_recv.at[half, p]).wait()
        block = x[j * group * frames : (j + 1) * group * frames].reshape(m, chan).astype(F32)
        qkv = dot((unit(block) * gain2).astype(BF16), wqkv[...]).astype(BF16)
        kbuf[j * m : (j + 1) * m] = qkv[:, chan : 2 * chan]
        vbuf[j * m : (j + 1) * m] = qkv[:, 2 * chan :]
        width = (j + 1) * m
        scores = lax.dot_general(
            qkv[:, :chan],
            kbuf[:width],
            (((1,), (1,)), ((), ())),
            preferred_element_type=F32,
        ) * chan ** (-0.5)
        query = lax.broadcasted_iota(jnp.int32, (m, width), 0) + j * m
        key = lax.broadcasted_iota(jnp.int32, (m, width), 1)
        seen = (lax.rem(query, per) == lax.rem(key, per)) & (key <= query)
        scores = jnp.where(seen, scores, -1e30)
        expo = jnp.where(seen, jnp.exp(scores - jnp.max(scores, axis=-1, keepdims=True)), 0.0)
        weights = (expo / jnp.sum(expo, axis=-1, keepdims=True)).astype(BF16)
        attended = dot(weights, vbuf[:width]).astype(BF16)
        mixed = (block + dot(attended, wo[...])).astype(BF16)
        mbuf[2 + j * group * frames : 2 + (j + 1) * group * frames] = mixed.reshape(
            group * frames, per, chan
        )
        for p in range(j * group, (j + 1) * group):
            start_to(return_copies(p), p)

    for p in range(n):
        r, c = place(p)
        landed = mext.at[:, r, c]
        pltpu.make_async_copy(landed, landed, b_recv.at[p]).wait()
    doubled = tbias[...].astype(F32).reshape(1, 2 * chan)
    for a in range(3):
        doubled = doubled + dot(mext[a : a + frames].reshape(-1, chan), tw[a])
    doubled = doubled.astype(BF16).reshape(frames, rows, cols, 2 * chan)
    for t in range(frames):
        out[2 * t] = doubled[t, :, :, :chan]
        out[2 * t + 1] = doubled[t, :, :, chan:]

    @pl.when(me < n - 1)
    def _():
        to_next.wait_send()

    to_row.wait_send()

    @pl.when(me > 0)
    def _():
        relay.wait_send()

    for p in range(n):
        send_done(scatter_copies(0, p), p)
        send_done(scatter_copies(1, p), p)
        send_done(return_copies(p), p)


def body(*args):
    latent = args[0]
    frames, rows, cols, chan = latent.shape
    n = lax.axis_size("tm")
    per = rows * cols // n
    tiled = per and per % 16 == 0 and cols % per == 0 and frames > 2
    if not tiled or lax.axis_size("row") != 2:
        return plain_body(*args)
    vmem, hbm = pl.BlockSpec(memory_space=pltpu.VMEM), pl.BlockSpec(memory_space=pl.ANY)
    total = n * frames
    return pl.pallas_call(
        functools.partial(window_kernel, n),
        out_shape=jax.ShapeDtypeStruct((2 * frames, rows, cols, chan), BF16),
        in_specs=[hbm, vmem, hbm, vmem, vmem, hbm, hbm, hbm, hbm, hbm, vmem],
        out_specs=vmem,
        scratch_shapes=[
            pltpu.VMEM((frames, rows, cols, chan), BF16),
            pltpu.VMEM((frames + 2, rows, cols, 3 * chan), BF16),
            pltpu.VMEM((frames + 2, cols, chan), BF16),
            pltpu.VMEM((3, 3 * chan, 3 * chan), BF16),
            pltpu.VMEM((frames, rows, cols, 3 * chan), F32),
            pltpu.VMEM((frames, rows, cols, chan), BF16),
            pltpu.VMEM((chan, 3 * chan), BF16),
            pltpu.VMEM((chan, chan), BF16),
            pltpu.VMEM((3, chan, 2 * chan), BF16),
            pltpu.VMEM((total, per, chan), BF16),
            pltpu.VMEM((total * per, chan), BF16),
            pltpu.VMEM((total * per, chan), BF16),
            pltpu.VMEM((total + 2, per, chan), BF16),
            pltpu.VMEM((frames + 2, rows, cols, chan), BF16),
            pltpu.SemaphoreType.DMA((6,)),
            pltpu.SemaphoreType.DMA((3, 9)),
            pltpu.SemaphoreType.DMA((3,)),
            pltpu.SemaphoreType.DMA((3,)),
            pltpu.SemaphoreType.DMA((2, n)),
            pltpu.SemaphoreType.DMA((2, n)),
            pltpu.SemaphoreType.DMA((n,)),
            pltpu.SemaphoreType.DMA((n,)),
        ],
        compiler_params=pltpu.CompilerParams(
            collective_id=0, has_side_effects=True, vmem_limit_bytes=48 * 1024 * 1024
        ),
    )(*args)


def solution(mesh):
    placed = (
        P(("groups", "tm"), "row", None, None),
        P(),
        P(),
        P(),
        P(),
        P(),
        P(),
        P(),
        P(),
        P(),
        P(),
    )
    return jax.shard_map(
        body,
        mesh=mesh,
        in_specs=placed,
        out_specs=P(("groups", "tm"), "row", None, None),
        check_vma=False,
    )
```

```python
import functools

import jax
import jax.numpy as jnp
from jax import lax
from jax.experimental import pallas as pl
from jax.experimental.pallas import tpu as pltpu
from jax.sharding import PartitionSpec as P


def shifted(value, axis, steps):
    count = lax.axis_size(axis)
    leading, last = (max(0, -steps), min(count, count - steps))
    return lax.ppermute(value, axis, [(source, source + steps) for source in range(leading, last)])


def with_halo(block, sides, width):
    for axis, dim in sides:
        count = lax.axis_size(axis)
        forward = [(i, i + 1) for i in range(count - 1)]
        backward = [(target, source) for source, target in forward]
        low = lax.ppermute(
            lax.slice_in_dim(block, block.shape[dim] - width, None, axis=dim), axis, forward
        )
        high = lax.ppermute(lax.slice_in_dim(block, 0, width, axis=dim), axis, backward)
        block = jnp.concatenate([low, block, high], axis=dim)
    return block


def channel_norm(values, gain):
    floats = values.astype(jnp.float32)
    return (
        floats
        * lax.rsqrt(jnp.mean(floats * floats, axis=-1, keepdims=True) + 1e-06)
        * gain.astype(jnp.float32)
    )


def attend(query, keys, values):
    frame_count = query.shape[0]
    channels = query.shape[2]
    scores = jnp.einsum(
        "tnc,snc->nts", query, keys, preferred_element_type=jnp.float32
    ) * channels ** (-0.5)
    later = lax.broadcasted_iota(jnp.int32, (frame_count, frame_count), 0)
    earlier = lax.broadcasted_iota(jnp.int32, (frame_count, frame_count), 1)
    causal_mask = (earlier <= later)[None]
    scores = jnp.where(causal_mask, scores, -1e30)
    highest = jnp.max(scores, axis=-1, keepdims=True)
    expo = jnp.where(causal_mask, jnp.exp(scores - highest), 0.0)
    weights = (expo / jnp.sum(expo, axis=-1, keepdims=True)).astype(jnp.bfloat16)
    return jnp.einsum("nts,snc->tnc", weights, values, preferred_element_type=jnp.float32).astype(
        jnp.bfloat16
    )


def flatten_block(block):
    return block.reshape(block.shape[0], block.shape[2], block.shape[3])


def plain_body(
    latent,
    conv_gain,
    conv_weight,
    conv_bias,
    attn_gain,
    w_query,
    w_key,
    w_value,
    w_out,
    time_weight,
    time_bias,
):
    frame_count, row_count, col_count, channels = latent.shape
    peers = lax.axis_size("tm")
    activated = jax.nn.silu(channel_norm(latent, conv_gain)).astype(jnp.bfloat16)
    carried = shifted(activated[frame_count - 2 :], "tm", 1)
    extended = jnp.concatenate([carried, activated], axis=0)
    padded = with_halo(extended, (("row", 1),), 1)
    padded = jnp.pad(padded, ((0, 0), (0, 0), (1, 1), (0, 0)))
    summed = jnp.zeros((frame_count * row_count * col_count, channels), jnp.float32)
    for offset in range(3):
        patches = jnp.concatenate(
            [
                padded[
                    offset : offset + frame_count,
                    row_offset : row_offset + row_count,
                    col_offset : col_offset + col_count,
                ]
                for row_offset in range(3)
                for col_offset in range(3)
            ],
            axis=-1,
        )
        summed = summed + jnp.dot(
            patches.reshape(-1, 9 * channels),
            conv_weight[offset].reshape(9 * channels, channels),
            preferred_element_type=jnp.float32,
        )
    hidden = (
        latent.astype(jnp.float32) + summed.reshape(latent.shape) + conv_bias.astype(jnp.float32)
    ).astype(jnp.bfloat16)
    attn_in = channel_norm(hidden, attn_gain).astype(jnp.bfloat16)
    positions = row_count * col_count
    per_peer = positions // peers
    blocked = attn_in.reshape(frame_count, peers, per_peer, channels)
    flat = flatten_block(lax.all_to_all(blocked, "tm", split_axis=1, concat_axis=0, tiled=True))
    stacked = flat.reshape(-1, channels)

    def project(matrix):
        return (
            jnp.dot(stacked, matrix, preferred_element_type=jnp.float32)
            .astype(jnp.bfloat16)
            .reshape(flat.shape)
        )

    attended = attend(project(w_query), project(w_key), project(w_value))[:, None]
    returned = lax.all_to_all(attended, "tm", split_axis=0, concat_axis=1, tiled=True)
    mixed_term = jnp.dot(
        returned.reshape(-1, channels), w_out, preferred_element_type=jnp.float32
    ).reshape(latent.shape)
    mixed = (hidden.astype(jnp.float32) + mixed_term).astype(jnp.bfloat16)
    mixed_cache = shifted(mixed[frame_count - 2 :], "tm", 1)
    mixed_ext = jnp.concatenate([mixed_cache, mixed], axis=0)
    doubled = jnp.zeros(
        (frame_count * row_count * col_count, 2 * channels), jnp.float32
    ) + time_bias.astype(jnp.float32)
    for offset in range(3):
        doubled = doubled + jnp.dot(
            mixed_ext[offset : offset + frame_count].reshape(-1, channels),
            time_weight[offset],
            preferred_element_type=jnp.float32,
        )
    doubled = doubled.reshape(frame_count, row_count, col_count, 2, channels).transpose(
        0, 3, 1, 2, 4
    )
    return doubled.reshape(2 * frame_count, row_count, col_count, channels).astype(jnp.bfloat16)


BF16, F32 = jnp.bfloat16, jnp.float32
MESH = pl.DeviceIdType.MESH


def unit(floats):
    return floats * lax.rsqrt(jnp.mean(floats * floats, axis=-1, keepdims=True) + 1e-06)


def dot(left, right):
    return jnp.dot(left, right, preferred_element_type=F32)


def window_kernel(
    n,
    latent_hbm,
    cgain_hbm,
    cw_hbm,
    cbias_hbm,
    again_hbm,
    wq_hbm,
    wk_hbm,
    wv_hbm,
    wo_hbm,
    tw_hbm,
    tbias_hbm,
    out,
    lat,
    lhs,
    rowh,
    cw,
    acc,
    hid,
    wqkv,
    wo,
    tw,
    x,
    kbuf,
    vbuf,
    mbuf,
    mext,
    cgain,
    cbias,
    again,
    tbias,
    load_sem,
    cw_sem,
    halo_send,
    halo_recv,
    a_send,
    a_recv,
    b_send,
    b_recv,
):
    frames, rows, cols, chan = lat.shape
    per = rows * cols // n
    own = frames * per
    me = lax.axis_index("tm")
    row = lax.axis_index("row")
    other = 1 - row

    loads = [pltpu.make_async_copy(latent_hbm, lat, load_sem.at[0])]
    for i, w in enumerate((wq_hbm, wk_hbm, wv_hbm)):
        loads.append(
            pltpu.make_async_copy(w, wqkv.at[:, pl.ds(i * chan, chan)], load_sem.at[1 + i])
        )
    loads.append(pltpu.make_async_copy(wo_hbm, wo, load_sem.at[4]))
    loads.append(pltpu.make_async_copy(again_hbm, again, load_sem.at[5]))
    loads.append(pltpu.make_async_copy(tbias_hbm, tbias, load_sem.at[6]))
    loads.append(pltpu.make_async_copy(tw_hbm, tw, load_sem.at[7]))
    gain_load = pltpu.make_async_copy(cgain_hbm, cgain, load_sem.at[8])
    bias_load = pltpu.make_async_copy(cbias_hbm, cbias, load_sem.at[9])
    cw_loads = {
        (a, b, e): pltpu.make_async_copy(
            cw_hbm.at[a, b, e],
            cw.at[a, pl.ds(b * chan, chan), pl.ds(e * chan, chan)],
            cw_sem.at[a, 3 * b + e],
        )
        for a in (2, 1, 0)
        for b in range(3)
        for e in range(3)
    }
    loads[0].start()
    gain_load.start()
    bias_load.start()
    for c in cw_loads.values():
        c.start()
    for c in loads[1:]:
        c.start()

    barrier = pltpu.get_barrier_semaphore()
    for k in range(1, n):
        pl.semaphore_signal(
            barrier, inc=1, device_id={"tm": lax.rem(me + k, n)}, device_id_type=MESH
        )
    pl.semaphore_signal(barrier, inc=1, device_id={"row": other}, device_id_type=MESH)

    loads[0].wait()
    gain_load.wait()
    bias_load.wait()
    gain = cgain[...].astype(F32).reshape(1, 1, 1, chan)
    normed = unit(lat[...].astype(F32)) * gain
    act = (normed / (1.0 + jnp.exp(-normed))).astype(BF16)
    mid = pl.ds(chan, chan)
    lhs[2:, :, :, chan : 2 * chan] = act

    pl.semaphore_wait(barrier, n)

    to_next = pltpu.make_async_remote_copy(
        lhs.at[pl.ds(frames, 2), :, :, mid],
        lhs.at[pl.ds(0, 2), :, :, mid],
        halo_send.at[0],
        halo_recv.at[0],
        device_id={"tm": jnp.minimum(me + 1, n - 1)},
        device_id_type=MESH,
    )
    to_row = pltpu.make_async_remote_copy(
        lhs.at[pl.ds(2, frames), other, :, mid],
        rowh.at[pl.ds(2, frames)],
        halo_send.at[1],
        halo_recv.at[1],
        device_id={"row": other},
        device_id_type=MESH,
    )
    relay = pltpu.make_async_remote_copy(
        lhs.at[pl.ds(0, 2), other, :, mid],
        rowh.at[pl.ds(0, 2)],
        halo_send.at[2],
        halo_recv.at[2],
        device_id={"row": other},
        device_id_type=MESH,
    )

    @pl.when(me < n - 1)
    def _():
        to_next.start()

    to_row.start()

    def spread(lo, hi):
        lhs[lo:hi, 1, :, 0:chan] = lhs[lo:hi, 0, :, chan : 2 * chan]
        lhs[lo:hi, 0, :, 2 * chan :] = lhs[lo:hi, 1, :, chan : 2 * chan]

    def edges(lo, hi):
        edge = rowh[lo:hi]
        lhs[lo:hi, 0, :, 0:chan] = jnp.where(row == 1, edge, jnp.zeros_like(edge))
        lhs[lo:hi, 1, :, 2 * chan :] = jnp.where(row == 0, edge, jnp.zeros_like(edge))

    spread(2, frames + 2)
    to_row.wait_recv()
    edges(2, frames + 2)

    def taps(lo, hi, a):
        part = lhs[lo:hi].reshape((hi - lo) * rows * cols, 3 * chan)
        return dot(part, cw[a]).reshape(hi - lo, rows, cols, 3 * chan)

    def loaded(a):
        for b in range(3):
            for e in range(3):
                cw_loads[a, b, e].wait()

    loaded(2)
    acc[...] = taps(2, frames + 2, 2)
    loaded(1)
    acc[1:] += taps(2, frames + 1, 1)
    loaded(0)
    acc[2:] += taps(2, frames, 0)

    bias = cbias[...].astype(F32).reshape(1, chan)

    def finish(lo, hi):
        m = (hi - lo) * rows * cols
        y = acc[lo:hi].reshape(m, 3 * chan)
        col = lax.rem(lax.broadcasted_iota(jnp.int32, (m, chan), 0), cols)
        left = jnp.where(col == 0, 0.0, pltpu.roll(y[:, :chan], 1, 0))
        right = jnp.where(col == cols - 1, 0.0, pltpu.roll(y[:, 2 * chan :], m - 1, 0))
        total = left + y[:, chan : 2 * chan] + right
        value = lat[lo:hi].astype(F32).reshape(m, chan) + total + bias
        hid[lo:hi] = value.astype(BF16).reshape(hi - lo, rows, cols, chan)

    def place(p):
        return p * per // cols, pl.ds(p * per % cols, per)

    def scatter_copies(half, p):
        lo, count = (2, frames - 2) if half == 0 else (0, 2)
        r, c = place(p)
        source = hid.at[pl.ds(lo, count), r, c]
        target = x.at[pl.ds(frames * me + lo, count)]
        remote = pltpu.make_async_remote_copy(
            source,
            target,
            a_send.at[half, p],
            a_recv.at[half, me],
            device_id={"tm": p},
            device_id_type=MESH,
        )
        local = pltpu.make_async_copy(source, target, a_recv.at[half, me])
        return remote, local

    def start_to(copies, p):
        remote, local = copies

        @pl.when(p != me)
        def _():
            remote.start()

        @pl.when(p == me)
        def _():
            local.start()

    def send_done(copies, p):
        remote = copies[0]

        @pl.when(p != me)
        def _():
            remote.wait_send()

    finish(2, frames)
    for p in range(n):
        start_to(scatter_copies(0, p), p)

    @pl.when(me > 0)
    def _():
        to_next.wait_recv()
        relay.start()

    @pl.when(me == 0)
    def _():
        lhs[0:2, :, :, chan : 2 * chan] = jnp.zeros((2, rows, cols, chan), BF16)
        rowh[0:2] = jnp.zeros((2, cols, chan), BF16)

    spread(0, 2)

    @pl.when(me > 0)
    def _():
        relay.wait_recv()

    edges(0, 2)
    acc[0:1] += taps(1, 2, 1)
    acc[0:2] += taps(0, 2, 0)
    finish(0, 2)
    for p in range(n):
        start_to(scatter_copies(1, p), p)

    for c in loads[1:]:
        c.wait()
    mbuf[0:2] = jnp.zeros((2, per, chan), BF16)
    gain2 = again[...].astype(F32).reshape(1, chan)

    def return_copies(p):
        r, c = place(0)
        first = me * per
        source = mbuf.at[pl.ds(frames * p, frames + 2)]
        target = mext.at[:, first // cols, pl.ds(pl.multiple_of(lax.rem(first, cols), per), per)]
        remote = pltpu.make_async_remote_copy(
            source,
            target,
            b_send.at[p],
            b_recv.at[me],
            device_id={"tm": p},
            device_id_type=MESH,
        )
        return remote, pltpu.make_async_copy(source, target, b_recv.at[me])

    group = 2 if n % 2 == 0 else 1
    m = group * own
    for j in range(n // group):
        for p in range(j * group, (j + 1) * group):
            for half, (lo, count) in enumerate(((2, frames - 2), (0, 2))):
                landed = x.at[pl.ds(frames * p + lo, count)]
                pltpu.make_async_copy(landed, landed, a_recv.at[half, p]).wait()
        block = x[j * group * frames : (j + 1) * group * frames].reshape(m, chan).astype(F32)
        qkv = dot((unit(block) * gain2).astype(BF16), wqkv[...]).astype(BF16)
        kbuf[j * m : (j + 1) * m] = qkv[:, chan : 2 * chan]
        vbuf[j * m : (j + 1) * m] = qkv[:, 2 * chan :]
        width = (j + 1) * m
        scores = lax.dot_general(
            qkv[:, :chan],
            kbuf[:width],
            (((1,), (1,)), ((), ())),
            preferred_element_type=F32,
        ) * chan ** (-0.5)
        query = lax.broadcasted_iota(jnp.int32, (m, width), 0) + j * m
        key = lax.broadcasted_iota(jnp.int32, (m, width), 1)
        seen = (lax.rem(query, per) == lax.rem(key, per)) & (key <= query)
        scores = jnp.where(seen, scores, -1e30)
        expo = jnp.where(seen, jnp.exp(scores - jnp.max(scores, axis=-1, keepdims=True)), 0.0)
        weights = (expo / jnp.sum(expo, axis=-1, keepdims=True)).astype(BF16)
        attended = dot(weights, vbuf[:width]).astype(BF16)
        mixed = (block + dot(attended, wo[...])).astype(BF16)
        mbuf[2 + j * group * frames : 2 + (j + 1) * group * frames] = mixed.reshape(
            group * frames, per, chan
        )
        for p in range(j * group, (j + 1) * group):
            start_to(return_copies(p), p)

    for p in range(n):
        r, c = place(p)
        landed = mext.at[:, r, c]
        pltpu.make_async_copy(landed, landed, b_recv.at[p]).wait()
    doubled = tbias[...].astype(F32).reshape(1, 2 * chan)
    for a in range(3):
        doubled = doubled + dot(mext[a : a + frames].reshape(-1, chan), tw[a])
    doubled = doubled.astype(BF16).reshape(frames, rows, cols, 2 * chan)
    for t in range(frames):
        out[2 * t] = doubled[t, :, :, :chan]
        out[2 * t + 1] = doubled[t, :, :, chan:]

    @pl.when(me < n - 1)
    def _():
        to_next.wait_send()

    to_row.wait_send()

    @pl.when(me > 0)
    def _():
        relay.wait_send()

    for p in range(n):
        send_done(scatter_copies(0, p), p)
        send_done(scatter_copies(1, p), p)
        send_done(return_copies(p), p)


def body(*args):
    latent = args[0]
    frames, rows, cols, chan = latent.shape
    n = lax.axis_size("tm")
    per = rows * cols // n
    tiled = per and per % 16 == 0 and cols % per == 0 and frames > 2
    if not tiled or lax.axis_size("row") != 2:
        return plain_body(*args)
    vmem, hbm = pl.BlockSpec(memory_space=pltpu.VMEM), pl.BlockSpec(memory_space=pltpu.HBM)
    total = n * frames
    return pl.pallas_call(
        functools.partial(window_kernel, n),
        out_shape=jax.ShapeDtypeStruct((2 * frames, rows, cols, chan), BF16),
        in_specs=[hbm] * 11,
        out_specs=vmem,
        scratch_shapes=[
            pltpu.VMEM((frames, rows, cols, chan), BF16),
            pltpu.VMEM((frames + 2, rows, cols, 3 * chan), BF16),
            pltpu.VMEM((frames + 2, cols, chan), BF16),
            pltpu.VMEM((3, 3 * chan, 3 * chan), BF16),
            pltpu.VMEM((frames, rows, cols, 3 * chan), F32),
            pltpu.VMEM((frames, rows, cols, chan), BF16),
            pltpu.VMEM((chan, 3 * chan), BF16),
            pltpu.VMEM((chan, chan), BF16),
            pltpu.VMEM((3, chan, 2 * chan), BF16),
            pltpu.VMEM((total, per, chan), BF16),
            pltpu.VMEM((total * per, chan), BF16),
            pltpu.VMEM((total * per, chan), BF16),
            pltpu.VMEM((total + 2, per, chan), BF16),
            pltpu.VMEM((frames + 2, rows, cols, chan), BF16),
            pltpu.VMEM((chan,), BF16),
            pltpu.VMEM((chan,), BF16),
            pltpu.VMEM((chan,), BF16),
            pltpu.VMEM((2 * chan,), BF16),
            pltpu.SemaphoreType.DMA((10,)),
            pltpu.SemaphoreType.DMA((3, 9)),
            pltpu.SemaphoreType.DMA((3,)),
            pltpu.SemaphoreType.DMA((3,)),
            pltpu.SemaphoreType.DMA((2, n)),
            pltpu.SemaphoreType.DMA((2, n)),
            pltpu.SemaphoreType.DMA((n,)),
            pltpu.SemaphoreType.DMA((n,)),
        ],
        compiler_params=pltpu.CompilerParams(
            collective_id=0, has_side_effects=True, vmem_limit_bytes=48 * 1024 * 1024
        ),
    )(*args)


def solution(mesh):
    placed = (
        P(("groups", "tm"), "row", None, None),
        P(),
        P(),
        P(),
        P(),
        P(),
        P(),
        P(),
        P(),
        P(),
        P(),
    )
    return jax.shard_map(
        body,
        mesh=mesh,
        in_specs=placed,
        out_specs=P(("groups", "tm"), "row", None, None),
        check_vma=False,
    )
```

```python
import functools

import jax
import jax.numpy as jnp
from jax import lax
from jax.experimental import pallas as pl
from jax.experimental.pallas import tpu as pltpu
from jax.sharding import PartitionSpec as P


def shifted(value, axis, steps):
    count = lax.axis_size(axis)
    leading, last = (max(0, -steps), min(count, count - steps))
    return lax.ppermute(value, axis, [(source, source + steps) for source in range(leading, last)])


def with_halo(block, sides, width):
    for axis, dim in sides:
        count = lax.axis_size(axis)
        forward = [(i, i + 1) for i in range(count - 1)]
        backward = [(target, source) for source, target in forward]
        low = lax.ppermute(
            lax.slice_in_dim(block, block.shape[dim] - width, None, axis=dim), axis, forward
        )
        high = lax.ppermute(lax.slice_in_dim(block, 0, width, axis=dim), axis, backward)
        block = jnp.concatenate([low, block, high], axis=dim)
    return block


def channel_norm(values, gain):
    floats = values.astype(jnp.float32)
    return (
        floats
        * lax.rsqrt(jnp.mean(floats * floats, axis=-1, keepdims=True) + 1e-06)
        * gain.astype(jnp.float32)
    )


def attend(query, keys, values):
    frame_count = query.shape[0]
    channels = query.shape[2]
    scores = jnp.einsum(
        "tnc,snc->nts", query, keys, preferred_element_type=jnp.float32
    ) * channels ** (-0.5)
    later = lax.broadcasted_iota(jnp.int32, (frame_count, frame_count), 0)
    earlier = lax.broadcasted_iota(jnp.int32, (frame_count, frame_count), 1)
    causal_mask = (earlier <= later)[None]
    scores = jnp.where(causal_mask, scores, -1e30)
    highest = jnp.max(scores, axis=-1, keepdims=True)
    expo = jnp.where(causal_mask, jnp.exp(scores - highest), 0.0)
    weights = (expo / jnp.sum(expo, axis=-1, keepdims=True)).astype(jnp.bfloat16)
    return jnp.einsum("nts,snc->tnc", weights, values, preferred_element_type=jnp.float32).astype(
        jnp.bfloat16
    )


def flatten_block(block):
    return block.reshape(block.shape[0], block.shape[2], block.shape[3])


def plain_body(
    latent,
    conv_gain,
    conv_weight,
    conv_bias,
    attn_gain,
    w_query,
    w_key,
    w_value,
    w_out,
    time_weight,
    time_bias,
):
    frame_count, row_count, col_count, channels = latent.shape
    peers = lax.axis_size("tm")
    activated = jax.nn.silu(channel_norm(latent, conv_gain)).astype(jnp.bfloat16)
    carried = shifted(activated[frame_count - 2 :], "tm", 1)
    extended = jnp.concatenate([carried, activated], axis=0)
    padded = with_halo(extended, (("row", 1),), 1)
    padded = jnp.pad(padded, ((0, 0), (0, 0), (1, 1), (0, 0)))
    summed = jnp.zeros((frame_count * row_count * col_count, channels), jnp.float32)
    for offset in range(3):
        patches = jnp.concatenate(
            [
                padded[
                    offset : offset + frame_count,
                    row_offset : row_offset + row_count,
                    col_offset : col_offset + col_count,
                ]
                for row_offset in range(3)
                for col_offset in range(3)
            ],
            axis=-1,
        )
        summed = summed + jnp.dot(
            patches.reshape(-1, 9 * channels),
            conv_weight[offset].reshape(9 * channels, channels),
            preferred_element_type=jnp.float32,
        )
    hidden = (
        latent.astype(jnp.float32) + summed.reshape(latent.shape) + conv_bias.astype(jnp.float32)
    ).astype(jnp.bfloat16)
    attn_in = channel_norm(hidden, attn_gain).astype(jnp.bfloat16)
    positions = row_count * col_count
    per_peer = positions // peers
    blocked = attn_in.reshape(frame_count, peers, per_peer, channels)
    flat = flatten_block(lax.all_to_all(blocked, "tm", split_axis=1, concat_axis=0, tiled=True))
    stacked = flat.reshape(-1, channels)

    def project(matrix):
        return (
            jnp.dot(stacked, matrix, preferred_element_type=jnp.float32)
            .astype(jnp.bfloat16)
            .reshape(flat.shape)
        )

    attended = attend(project(w_query), project(w_key), project(w_value))[:, None]
    returned = lax.all_to_all(attended, "tm", split_axis=0, concat_axis=1, tiled=True)
    mixed_term = jnp.dot(
        returned.reshape(-1, channels), w_out, preferred_element_type=jnp.float32
    ).reshape(latent.shape)
    mixed = (hidden.astype(jnp.float32) + mixed_term).astype(jnp.bfloat16)
    mixed_cache = shifted(mixed[frame_count - 2 :], "tm", 1)
    mixed_ext = jnp.concatenate([mixed_cache, mixed], axis=0)
    doubled = jnp.zeros(
        (frame_count * row_count * col_count, 2 * channels), jnp.float32
    ) + time_bias.astype(jnp.float32)
    for offset in range(3):
        doubled = doubled + jnp.dot(
            mixed_ext[offset : offset + frame_count].reshape(-1, channels),
            time_weight[offset],
            preferred_element_type=jnp.float32,
        )
    doubled = doubled.reshape(frame_count, row_count, col_count, 2, channels).transpose(
        0, 3, 1, 2, 4
    )
    return doubled.reshape(2 * frame_count, row_count, col_count, channels).astype(jnp.bfloat16)


BF16, F32 = jnp.bfloat16, jnp.float32
MESH = pl.DeviceIdType.MESH


def unit(floats):
    return floats * lax.rsqrt(jnp.mean(floats * floats, axis=-1, keepdims=True) + 1e-06)


def dot(left, right):
    return jnp.dot(left, right, preferred_element_type=F32)


def window_kernel(
    n,
    latent_hbm,
    cgain_hbm,
    cw_hbm,
    cbias_hbm,
    again_hbm,
    wq_hbm,
    wk_hbm,
    wv_hbm,
    wo_hbm,
    tw_hbm,
    tbias_hbm,
    out,
    lat,
    lhs,
    rowh,
    cw,
    acc,
    hid,
    wqkv,
    wo,
    tw,
    x,
    kbuf,
    vbuf,
    mbuf,
    mext,
    cgain,
    cbias,
    again,
    tbias,
    load_sem,
    cw_sem,
    halo_send,
    halo_recv,
    a_send,
    a_recv,
    b_send,
    b_recv,
):
    frames, rows, cols, chan = lat.shape
    per = rows * cols // n
    own = frames * per
    me = lax.axis_index("tm")
    row = lax.axis_index("row")
    other = 1 - row

    loads = [pltpu.make_async_copy(latent_hbm, lat, load_sem.at[0])]
    for i, w in enumerate((wq_hbm, wk_hbm, wv_hbm)):
        loads.append(
            pltpu.make_async_copy(w, wqkv.at[:, pl.ds(i * chan, chan)], load_sem.at[1 + i])
        )
    loads.append(pltpu.make_async_copy(wo_hbm, wo, load_sem.at[4]))
    loads.append(pltpu.make_async_copy(again_hbm, again, load_sem.at[5]))
    loads.append(pltpu.make_async_copy(tbias_hbm, tbias, load_sem.at[6]))
    loads.append(pltpu.make_async_copy(tw_hbm, tw, load_sem.at[7]))
    gain_load = pltpu.make_async_copy(cgain_hbm, cgain, load_sem.at[8])
    bias_load = pltpu.make_async_copy(cbias_hbm, cbias, load_sem.at[9])
    cw_loads = {
        (a, b, e): pltpu.make_async_copy(
            cw_hbm.at[a, b, e],
            cw.at[a, pl.ds(b * chan, chan), pl.ds(e * chan, chan)],
            cw_sem.at[a, 3 * b + e],
        )
        for a in (2, 1, 0)
        for b in range(3)
        for e in range(3)
    }
    loads[0].start()
    gain_load.start()
    bias_load.start()
    for c in cw_loads.values():
        c.start()
    for c in loads[1:]:
        c.start()

    barrier = pltpu.get_barrier_semaphore()
    for k in range(1, n):
        pl.semaphore_signal(
            barrier, inc=1, device_id={"tm": lax.rem(me + k, n)}, device_id_type=MESH
        )
    pl.semaphore_signal(barrier, inc=1, device_id={"row": other}, device_id_type=MESH)

    loads[0].wait()
    gain_load.wait()
    bias_load.wait()
    gain = cgain[...].astype(F32).reshape(1, 1, 1, chan)
    normed = unit(lat[...].astype(F32)) * gain
    act = (normed / (1.0 + jnp.exp(-normed))).astype(BF16)
    mid = pl.ds(chan, chan)
    lhs[2:, :, :, chan : 2 * chan] = act

    pl.semaphore_wait(barrier, n)

    to_next = pltpu.make_async_remote_copy(
        lhs.at[pl.ds(frames, 2), :, :, mid],
        lhs.at[pl.ds(0, 2), :, :, mid],
        halo_send.at[0],
        halo_recv.at[0],
        device_id={"tm": jnp.minimum(me + 1, n - 1)},
        device_id_type=MESH,
    )
    to_row = pltpu.make_async_remote_copy(
        lhs.at[pl.ds(2, frames), other, :, mid],
        rowh.at[pl.ds(2, frames)],
        halo_send.at[1],
        halo_recv.at[1],
        device_id={"row": other},
        device_id_type=MESH,
    )
    relay = pltpu.make_async_remote_copy(
        lhs.at[pl.ds(0, 2), other, :, mid],
        rowh.at[pl.ds(0, 2)],
        halo_send.at[2],
        halo_recv.at[2],
        device_id={"row": other},
        device_id_type=MESH,
    )

    @pl.when(me < n - 1)
    def _():
        to_next.start()

    to_row.start()

    def spread(lo, hi):
        lhs[lo:hi, 1, :, 0:chan] = lhs[lo:hi, 0, :, chan : 2 * chan]
        lhs[lo:hi, 0, :, 2 * chan :] = lhs[lo:hi, 1, :, chan : 2 * chan]

    def edges(lo, hi):
        edge = rowh[lo:hi]
        lhs[lo:hi, 0, :, 0:chan] = jnp.where(row == 1, edge, jnp.zeros_like(edge))
        lhs[lo:hi, 1, :, 2 * chan :] = jnp.where(row == 0, edge, jnp.zeros_like(edge))

    spread(2, frames + 2)
    to_row.wait_recv()
    edges(2, frames + 2)

    def taps(lo, hi, a):
        part = lhs[lo:hi].reshape((hi - lo) * rows * cols, 3 * chan)
        return dot(part, cw[a]).reshape(hi - lo, rows, cols, 3 * chan)

    def loaded(a):
        for b in range(3):
            for e in range(3):
                cw_loads[a, b, e].wait()

    loaded(2)
    acc[...] = taps(2, frames + 2, 2)
    loaded(1)
    acc[1:] += taps(2, frames + 1, 1)
    loaded(0)
    acc[2:] += taps(2, frames, 0)

    bias = cbias[...].astype(F32).reshape(1, chan)

    def finish(lo, hi):
        m = (hi - lo) * rows * cols
        y = acc[lo:hi].reshape(m, 3 * chan)
        col = lax.rem(lax.broadcasted_iota(jnp.int32, (m, chan), 0), cols)
        left = jnp.where(col == 0, 0.0, pltpu.roll(y[:, :chan], 1, 0))
        right = jnp.where(col == cols - 1, 0.0, pltpu.roll(y[:, 2 * chan :], m - 1, 0))
        total = left + y[:, chan : 2 * chan] + right
        value = lat[lo:hi].astype(F32).reshape(m, chan) + total + bias
        hid[lo:hi] = value.astype(BF16).reshape(hi - lo, rows, cols, chan)

    def place(p):
        return p * per // cols, pl.ds(p * per % cols, per)

    def scatter_copies(half, p):
        lo, count = (2, frames - 2) if half == 0 else (0, 2)
        r, c = place(p)
        source = hid.at[pl.ds(lo, count), r, c]
        target = x.at[pl.ds(frames * me + lo, count)]
        remote = pltpu.make_async_remote_copy(
            source,
            target,
            a_send.at[half, p],
            a_recv.at[half, me],
            device_id={"tm": p},
            device_id_type=MESH,
        )
        local = pltpu.make_async_copy(source, target, a_recv.at[half, me])
        return remote, local

    def start_to(copies, p):
        remote, local = copies

        @pl.when(p != me)
        def _():
            remote.start()

        @pl.when(p == me)
        def _():
            local.start()

    def send_done(copies, p):
        remote = copies[0]

        @pl.when(p != me)
        def _():
            remote.wait_send()

    finish(2, frames)
    for p in range(n):
        start_to(scatter_copies(0, p), p)

    @pl.when(me > 0)
    def _():
        to_next.wait_recv()
        relay.start()

    @pl.when(me == 0)
    def _():
        lhs[0:2, :, :, chan : 2 * chan] = jnp.zeros((2, rows, cols, chan), BF16)
        rowh[0:2] = jnp.zeros((2, cols, chan), BF16)

    spread(0, 2)

    @pl.when(me > 0)
    def _():
        relay.wait_recv()

    edges(0, 2)
    acc[0:1] += taps(1, 2, 1)
    acc[0:2] += taps(0, 2, 0)
    finish(0, 2)
    for p in range(n):
        start_to(scatter_copies(1, p), p)

    for c in loads[1:]:
        c.wait()
    mbuf[0:2] = jnp.zeros((2, per, chan), BF16)
    gain2 = again[...].astype(F32).reshape(1, chan)

    def return_copies(p):
        r, c = place(0)
        first = me * per
        source = mbuf.at[pl.ds(frames * p, frames + 2)]
        target = mext.at[:, first // cols, pl.ds(pl.multiple_of(lax.rem(first, cols), per), per)]
        remote = pltpu.make_async_remote_copy(
            source,
            target,
            b_send.at[p],
            b_recv.at[me],
            device_id={"tm": p},
            device_id_type=MESH,
        )
        return remote, pltpu.make_async_copy(source, target, b_recv.at[me])

    group = 2 if n % 2 == 0 else 1
    m = group * own
    for j in range(n // group):
        for p in range(j * group, (j + 1) * group):
            for half, (lo, count) in enumerate(((2, frames - 2), (0, 2))):
                landed = x.at[pl.ds(frames * p + lo, count)]
                pltpu.make_async_copy(landed, landed, a_recv.at[half, p]).wait()
        block = x[j * group * frames : (j + 1) * group * frames].reshape(m, chan).astype(F32)
        qkv = dot((unit(block) * gain2).astype(BF16), wqkv[...]).astype(BF16)
        kbuf[j * m : (j + 1) * m] = qkv[:, chan : 2 * chan]
        vbuf[j * m : (j + 1) * m] = qkv[:, 2 * chan :]
        width = (j + 1) * m
        scores = lax.dot_general(
            qkv[:, :chan],
            kbuf[:width],
            (((1,), (1,)), ((), ())),
            preferred_element_type=F32,
        ) * chan ** (-0.5)
        query = lax.broadcasted_iota(jnp.int32, (m, width), 0) + j * m
        key = lax.broadcasted_iota(jnp.int32, (m, width), 1)
        seen = (lax.rem(query, per) == lax.rem(key, per)) & (key <= query)
        scores = jnp.where(seen, scores, -1e30)
        expo = jnp.where(seen, jnp.exp(scores - jnp.max(scores, axis=-1, keepdims=True)), 0.0)
        weights = (expo / jnp.sum(expo, axis=-1, keepdims=True)).astype(BF16)
        attended = dot(weights, vbuf[:width]).astype(BF16)
        mixed = (block + dot(attended, wo[...])).astype(BF16)
        mbuf[2 + j * group * frames : 2 + (j + 1) * group * frames] = mixed.reshape(
            group * frames, per, chan
        )
        for p in range(j * group, (j + 1) * group):
            start_to(return_copies(p), p)

    for p in range(n):
        r, c = place(p)
        landed = mext.at[:, r, c]
        pltpu.make_async_copy(landed, landed, b_recv.at[p]).wait()
    doubled = tbias[...].astype(F32).reshape(1, 2 * chan)
    for a in range(3):
        doubled = doubled + dot(mext[a : a + frames].reshape(-1, chan), tw[a])
    doubled = doubled.astype(BF16).reshape(frames, rows, cols, 2 * chan)
    for t in range(frames):
        out[2 * t] = doubled[t, :, :, :chan]
        out[2 * t + 1] = doubled[t, :, :, chan:]

    @pl.when(me < n - 1)
    def _():
        to_next.wait_send()

    to_row.wait_send()

    @pl.when(me > 0)
    def _():
        relay.wait_send()

    for p in range(n):
        send_done(scatter_copies(0, p), p)
        send_done(scatter_copies(1, p), p)
        send_done(return_copies(p), p)


def body(*args):
    latent = args[0]
    frames, rows, cols, chan = latent.shape
    n = lax.axis_size("tm")
    per = rows * cols // n
    tiled = per and per % 16 == 0 and cols % per == 0 and frames > 2
    if not tiled or lax.axis_size("row") != 2:
        return plain_body(*args)
    vmem, hbm = pl.BlockSpec(memory_space=pltpu.VMEM), pl.BlockSpec(memory_space=pltpu.HBM)
    total = n * frames
    return pl.pallas_call(
        functools.partial(window_kernel, n),
        out_shape=jax.ShapeDtypeStruct((2 * frames, rows, cols, chan), BF16),
        in_specs=[hbm] * 11,
        out_specs=vmem,
        scratch_shapes=[
            pltpu.VMEM((frames, rows, cols, chan), BF16),
            pltpu.VMEM((frames + 2, rows, cols, 3 * chan), BF16),
            pltpu.VMEM((frames + 2, cols, chan), BF16),
            pltpu.VMEM((3, 3 * chan, 3 * chan), BF16),
            pltpu.VMEM((frames, rows, cols, 3 * chan), F32),
            pltpu.VMEM((frames, rows, cols, chan), BF16),
            pltpu.VMEM((chan, 3 * chan), BF16),
            pltpu.VMEM((chan, chan), BF16),
            pltpu.VMEM((3, chan, 2 * chan), BF16),
            pltpu.VMEM((total, per, chan), BF16),
            pltpu.VMEM((total * per, chan), BF16),
            pltpu.VMEM((total * per, chan), BF16),
            pltpu.VMEM((total + 2, per, chan), BF16),
            pltpu.VMEM((frames + 2, rows, cols, chan), BF16),
            pltpu.VMEM((chan,), BF16),
            pltpu.VMEM((chan,), BF16),
            pltpu.VMEM((chan,), BF16),
            pltpu.VMEM((2 * chan,), BF16),
            pltpu.SemaphoreType.DMA((10,)),
            pltpu.SemaphoreType.DMA((3, 9)),
            pltpu.SemaphoreType.DMA((3,)),
            pltpu.SemaphoreType.DMA((3,)),
            pltpu.SemaphoreType.DMA((2, n)),
            pltpu.SemaphoreType.DMA((2, n)),
            pltpu.SemaphoreType.DMA((n,)),
            pltpu.SemaphoreType.DMA((n,)),
        ],
        compiler_params=pltpu.CompilerParams(
            collective_id=0, has_side_effects=True, vmem_limit_bytes=56 * 1024 * 1024
        ),
    )(*args)


def solution(mesh):
    placed = (
        P(("groups", "tm"), "row", None, None),
        P(),
        P(),
        P(),
        P(),
        P(),
        P(),
        P(),
        P(),
        P(),
        P(),
    )
    return jax.shard_map(
        body,
        mesh=mesh,
        in_specs=placed,
        out_specs=P(("groups", "tm"), "row", None, None),
        check_vma=False,
    )
```

```python
import functools

import jax
import jax.numpy as jnp
from jax import lax
from jax.experimental import pallas as pl
from jax.experimental.pallas import tpu as pltpu
from jax.sharding import PartitionSpec as P


def shifted(value, axis, steps):
    count = lax.axis_size(axis)
    leading, last = (max(0, -steps), min(count, count - steps))
    return lax.ppermute(value, axis, [(source, source + steps) for source in range(leading, last)])


def with_halo(block, sides, width):
    for axis, dim in sides:
        count = lax.axis_size(axis)
        forward = [(i, i + 1) for i in range(count - 1)]
        backward = [(target, source) for source, target in forward]
        low = lax.ppermute(
            lax.slice_in_dim(block, block.shape[dim] - width, None, axis=dim), axis, forward
        )
        high = lax.ppermute(lax.slice_in_dim(block, 0, width, axis=dim), axis, backward)
        block = jnp.concatenate([low, block, high], axis=dim)
    return block


def channel_norm(values, gain):
    floats = values.astype(jnp.float32)
    return (
        floats
        * lax.rsqrt(jnp.mean(floats * floats, axis=-1, keepdims=True) + 1e-06)
        * gain.astype(jnp.float32)
    )


def attend(query, keys, values):
    frame_count = query.shape[0]
    channels = query.shape[2]
    scores = jnp.einsum(
        "tnc,snc->nts", query, keys, preferred_element_type=jnp.float32
    ) * channels ** (-0.5)
    later = lax.broadcasted_iota(jnp.int32, (frame_count, frame_count), 0)
    earlier = lax.broadcasted_iota(jnp.int32, (frame_count, frame_count), 1)
    causal_mask = (earlier <= later)[None]
    scores = jnp.where(causal_mask, scores, -1e30)
    highest = jnp.max(scores, axis=-1, keepdims=True)
    expo = jnp.where(causal_mask, jnp.exp(scores - highest), 0.0)
    weights = (expo / jnp.sum(expo, axis=-1, keepdims=True)).astype(jnp.bfloat16)
    return jnp.einsum("nts,snc->tnc", weights, values, preferred_element_type=jnp.float32).astype(
        jnp.bfloat16
    )


def flatten_block(block):
    return block.reshape(block.shape[0], block.shape[2], block.shape[3])


def plain_body(
    latent,
    conv_gain,
    conv_weight,
    conv_bias,
    attn_gain,
    w_query,
    w_key,
    w_value,
    w_out,
    time_weight,
    time_bias,
):
    frame_count, row_count, col_count, channels = latent.shape
    peers = lax.axis_size("tm")
    activated = jax.nn.silu(channel_norm(latent, conv_gain)).astype(jnp.bfloat16)
    carried = shifted(activated[frame_count - 2 :], "tm", 1)
    extended = jnp.concatenate([carried, activated], axis=0)
    padded = with_halo(extended, (("row", 1),), 1)
    padded = jnp.pad(padded, ((0, 0), (0, 0), (1, 1), (0, 0)))
    summed = jnp.zeros((frame_count * row_count * col_count, channels), jnp.float32)
    for offset in range(3):
        patches = jnp.concatenate(
            [
                padded[
                    offset : offset + frame_count,
                    row_offset : row_offset + row_count,
                    col_offset : col_offset + col_count,
                ]
                for row_offset in range(3)
                for col_offset in range(3)
            ],
            axis=-1,
        )
        summed = summed + jnp.dot(
            patches.reshape(-1, 9 * channels),
            conv_weight[offset].reshape(9 * channels, channels),
            preferred_element_type=jnp.float32,
        )
    hidden = (
        latent.astype(jnp.float32) + summed.reshape(latent.shape) + conv_bias.astype(jnp.float32)
    ).astype(jnp.bfloat16)
    attn_in = channel_norm(hidden, attn_gain).astype(jnp.bfloat16)
    positions = row_count * col_count
    per_peer = positions // peers
    blocked = attn_in.reshape(frame_count, peers, per_peer, channels)
    flat = flatten_block(lax.all_to_all(blocked, "tm", split_axis=1, concat_axis=0, tiled=True))
    stacked = flat.reshape(-1, channels)

    def project(matrix):
        return (
            jnp.dot(stacked, matrix, preferred_element_type=jnp.float32)
            .astype(jnp.bfloat16)
            .reshape(flat.shape)
        )

    attended = attend(project(w_query), project(w_key), project(w_value))[:, None]
    returned = lax.all_to_all(attended, "tm", split_axis=0, concat_axis=1, tiled=True)
    mixed_term = jnp.dot(
        returned.reshape(-1, channels), w_out, preferred_element_type=jnp.float32
    ).reshape(latent.shape)
    mixed = (hidden.astype(jnp.float32) + mixed_term).astype(jnp.bfloat16)
    mixed_cache = shifted(mixed[frame_count - 2 :], "tm", 1)
    mixed_ext = jnp.concatenate([mixed_cache, mixed], axis=0)
    doubled = jnp.zeros(
        (frame_count * row_count * col_count, 2 * channels), jnp.float32
    ) + time_bias.astype(jnp.float32)
    for offset in range(3):
        doubled = doubled + jnp.dot(
            mixed_ext[offset : offset + frame_count].reshape(-1, channels),
            time_weight[offset],
            preferred_element_type=jnp.float32,
        )
    doubled = doubled.reshape(frame_count, row_count, col_count, 2, channels).transpose(
        0, 3, 1, 2, 4
    )
    return doubled.reshape(2 * frame_count, row_count, col_count, channels).astype(jnp.bfloat16)


BF16, F32 = jnp.bfloat16, jnp.float32
MESH = pl.DeviceIdType.MESH


def unit(floats):
    return floats * lax.rsqrt(jnp.mean(floats * floats, axis=-1, keepdims=True) + 1e-06)


def dot(left, right):
    return jnp.dot(left, right, preferred_element_type=F32)


def window_kernel(
    n,
    latent_hbm,
    cgain_hbm,
    cw_hbm,
    cbias_hbm,
    again_hbm,
    wq_hbm,
    wk_hbm,
    wv_hbm,
    wo_hbm,
    tw_hbm,
    tbias_hbm,
    out,
    lat,
    lhs,
    rowh,
    cw,
    acc,
    hid,
    wqkv,
    wo,
    tw,
    x,
    kbuf,
    vbuf,
    mbuf,
    mext,
    cgain,
    cbias,
    again,
    tbias,
    load_sem,
    cw_sem,
    halo_send,
    halo_recv,
    a_send,
    a_recv,
    b_send,
    b_recv,
):
    frames, rows, cols, chan = lat.shape
    per = rows * cols // n
    own = frames * per
    me = lax.axis_index("tm")
    row = lax.axis_index("row")
    other = 1 - row

    loads = [pltpu.make_async_copy(latent_hbm, lat, load_sem.at[0])]
    for i, w in enumerate((wq_hbm, wk_hbm, wv_hbm)):
        loads.append(
            pltpu.make_async_copy(w, wqkv.at[:, pl.ds(i * chan, chan)], load_sem.at[1 + i])
        )
    loads.append(pltpu.make_async_copy(wo_hbm, wo, load_sem.at[4]))
    loads.append(pltpu.make_async_copy(again_hbm, again, load_sem.at[5]))
    loads.append(pltpu.make_async_copy(tbias_hbm, tbias, load_sem.at[6]))
    loads.append(pltpu.make_async_copy(tw_hbm, tw, load_sem.at[7]))
    gain_load = pltpu.make_async_copy(cgain_hbm, cgain, load_sem.at[8])
    bias_load = pltpu.make_async_copy(cbias_hbm, cbias, load_sem.at[9])
    cw_loads = {
        (a, b, e): pltpu.make_async_copy(
            cw_hbm.at[a, b, e],
            cw.at[a, pl.ds(b * chan, chan), pl.ds(e * chan, chan)],
            cw_sem.at[a, 3 * b + e],
        )
        for a in (2, 1, 0)
        for b in range(3)
        for e in range(3)
    }
    loads[0].start()
    gain_load.start()
    bias_load.start()
    for c in cw_loads.values():
        c.start()
    for c in loads[1:]:
        c.start()

    barrier = pltpu.get_barrier_semaphore()
    for k in range(1, n):
        pl.semaphore_signal(
            barrier, inc=1, device_id={"tm": lax.rem(me + k, n)}, device_id_type=MESH
        )
    pl.semaphore_signal(barrier, inc=1, device_id={"row": other}, device_id_type=MESH)

    loads[0].wait()
    gain_load.wait()
    bias_load.wait()
    gain = cgain[...].astype(F32).reshape(1, 1, 1, chan)
    normed = unit(lat[...].astype(F32)) * gain
    act = (normed / (1.0 + jnp.exp(-normed))).astype(BF16)
    mid = pl.ds(chan, chan)
    lhs[2:, :, :, chan : 2 * chan] = act

    pl.semaphore_wait(barrier, n)

    to_next = pltpu.make_async_remote_copy(
        lhs.at[pl.ds(frames, 2), :, :, mid],
        lhs.at[pl.ds(0, 2), :, :, mid],
        halo_send.at[0],
        halo_recv.at[0],
        device_id={"tm": jnp.minimum(me + 1, n - 1)},
        device_id_type=MESH,
    )
    to_row = pltpu.make_async_remote_copy(
        lhs.at[pl.ds(2, frames), other, :, mid],
        rowh.at[pl.ds(2, frames)],
        halo_send.at[1],
        halo_recv.at[1],
        device_id={"row": other},
        device_id_type=MESH,
    )
    relay = pltpu.make_async_remote_copy(
        lhs.at[pl.ds(0, 2), other, :, mid],
        rowh.at[pl.ds(0, 2)],
        halo_send.at[2],
        halo_recv.at[2],
        device_id={"row": other},
        device_id_type=MESH,
    )

    @pl.when(me < n - 1)
    def _():
        to_next.start()

    to_row.start()

    def spread(lo, hi):
        lhs[lo:hi, 1, :, 0:chan] = lhs[lo:hi, 0, :, chan : 2 * chan]
        lhs[lo:hi, 0, :, 2 * chan :] = lhs[lo:hi, 1, :, chan : 2 * chan]

    def edges(lo, hi):
        edge = rowh[lo:hi]
        lhs[lo:hi, 0, :, 0:chan] = jnp.where(row == 1, edge, jnp.zeros_like(edge))
        lhs[lo:hi, 1, :, 2 * chan :] = jnp.where(row == 0, edge, jnp.zeros_like(edge))

    spread(2, frames + 2)
    to_row.wait_recv()
    edges(2, frames + 2)

    def taps(lo, hi, a):
        part = lhs[lo:hi].reshape((hi - lo) * rows * cols, 3 * chan)
        return dot(part, cw[a]).reshape(hi - lo, rows, cols, 3 * chan)

    def loaded(a):
        for b in range(3):
            for e in range(3):
                cw_loads[a, b, e].wait()

    loaded(2)
    acc[...] = taps(2, frames + 2, 2)
    loaded(1)
    acc[1:] += taps(2, frames + 1, 1)
    loaded(0)
    acc[2:] += taps(2, frames, 0)

    bias = cbias[...].astype(F32).reshape(1, chan)

    def finish(lo, hi):
        m = (hi - lo) * rows * cols
        y = acc[lo:hi].reshape(m, 3 * chan)
        col = lax.rem(lax.broadcasted_iota(jnp.int32, (m, chan), 0), cols)
        left = jnp.where(col == 0, 0.0, pltpu.roll(y[:, :chan], 1, 0))
        right = jnp.where(col == cols - 1, 0.0, pltpu.roll(y[:, 2 * chan :], m - 1, 0))
        total = left + y[:, chan : 2 * chan] + right
        value = lat[lo:hi].astype(F32).reshape(m, chan) + total + bias
        hid[lo:hi] = value.astype(BF16).reshape(hi - lo, rows, cols, chan)

    def place(p):
        return p * per // cols, pl.ds(p * per % cols, per)

    def turned(p):
        first = p * per
        return first // cols, pl.ds(pl.multiple_of(lax.rem(first, cols), per), per)

    order = sorted(range(n), key=lambda k: -min(k, n - k))

    def start_copy(source, target, send, recv, k, p):
        if k == 0:
            pltpu.make_async_copy(source, target, recv).start()
        else:
            pltpu.make_async_remote_copy(
                source,
                target,
                send,
                recv,
                device_id={"tm": p},
                device_id_type=MESH,
            ).start()

    def scatter(half):
        lo, count = (2, frames - 2) if half == 0 else (0, 2)
        for k in order:
            p = lax.rem(me + k, n)
            r, c = turned(p)
            start_copy(
                hid.at[pl.ds(lo, count), r, c],
                x.at[pl.ds(frames * me + lo, count)],
                a_send.at[half, k],
                a_recv.at[half, me],
                k,
                p,
            )

    finish(2, frames)
    scatter(0)

    @pl.when(me > 0)
    def _():
        to_next.wait_recv()
        relay.start()

    @pl.when(me == 0)
    def _():
        lhs[0:2, :, :, chan : 2 * chan] = jnp.zeros((2, rows, cols, chan), BF16)
        rowh[0:2] = jnp.zeros((2, cols, chan), BF16)

    spread(0, 2)

    @pl.when(me > 0)
    def _():
        relay.wait_recv()

    edges(0, 2)
    acc[0:1] += taps(1, 2, 1)
    acc[0:2] += taps(0, 2, 0)
    finish(0, 2)
    scatter(1)

    for c in loads[1:]:
        c.wait()
    mbuf[0:2] = jnp.zeros((2, per, chan), BF16)
    gain2 = again[...].astype(F32).reshape(1, chan)

    group = 2 if n % 2 == 0 else 1
    m = group * own
    for j in range(n // group):
        for p in range(j * group, (j + 1) * group):
            for half, (lo, count) in enumerate(((2, frames - 2), (0, 2))):
                landed = x.at[pl.ds(frames * p + lo, count)]
                pltpu.make_async_copy(landed, landed, a_recv.at[half, p]).wait()
        block = x[j * group * frames : (j + 1) * group * frames].reshape(m, chan).astype(F32)
        qkv = dot((unit(block) * gain2).astype(BF16), wqkv[...]).astype(BF16)
        kbuf[j * m : (j + 1) * m] = qkv[:, chan : 2 * chan]
        vbuf[j * m : (j + 1) * m] = qkv[:, 2 * chan :]
        width = (j + 1) * m
        scores = lax.dot_general(
            qkv[:, :chan],
            kbuf[:width],
            (((1,), (1,)), ((), ())),
            preferred_element_type=F32,
        ) * chan ** (-0.5)
        query = lax.broadcasted_iota(jnp.int32, (m, width), 0) + j * m
        key = lax.broadcasted_iota(jnp.int32, (m, width), 1)
        seen = (lax.rem(query, per) == lax.rem(key, per)) & (key <= query)
        scores = jnp.where(seen, scores, -1e30)
        expo = jnp.where(seen, jnp.exp(scores - jnp.max(scores, axis=-1, keepdims=True)), 0.0)
        weights = (expo / jnp.sum(expo, axis=-1, keepdims=True)).astype(BF16)
        attended = dot(weights, vbuf[:width]).astype(BF16)
        mixed = (block + dot(attended, wo[...])).astype(BF16)
        mbuf[2 + j * group * frames : 2 + (j + 1) * group * frames] = mixed.reshape(
            group * frames, per, chan
        )

    r, c = turned(me)
    for k in order:
        p = lax.rem(me + k, n)
        start_copy(
            mbuf.at[pl.ds(frames * p, frames + 2)],
            mext.at[:, r, c],
            b_send.at[k],
            b_recv.at[me],
            k,
            p,
        )

    for p in range(n):
        r, c = place(p)
        landed = mext.at[:, r, c]
        pltpu.make_async_copy(landed, landed, b_recv.at[p]).wait()
    doubled = tbias[...].astype(F32).reshape(1, 2 * chan)
    for a in range(3):
        doubled = doubled + dot(mext[a : a + frames].reshape(-1, chan), tw[a])
    doubled = doubled.astype(BF16).reshape(frames, rows, cols, 2 * chan)
    for t in range(frames):
        out[2 * t] = doubled[t, :, :, :chan]
        out[2 * t + 1] = doubled[t, :, :, chan:]

    @pl.when(me < n - 1)
    def _():
        to_next.wait_send()

    to_row.wait_send()

    @pl.when(me > 0)
    def _():
        relay.wait_send()

    for k in range(1, n):
        for half, count in enumerate((frames - 2, 2)):
            sent = hid.at[pl.ds(0, count), 0, pl.ds(0, per)]
            pltpu.make_async_copy(sent, sent, a_send.at[half, k]).wait()
        sent = mbuf.at[pl.ds(0, frames + 2)]
        pltpu.make_async_copy(sent, sent, b_send.at[k]).wait()


def body(*args):
    latent = args[0]
    frames, rows, cols, chan = latent.shape
    n = lax.axis_size("tm")
    per = rows * cols // n
    tiled = per and per % 16 == 0 and cols % per == 0 and frames > 2
    if not tiled or lax.axis_size("row") != 2:
        return plain_body(*args)
    vmem, hbm = pl.BlockSpec(memory_space=pltpu.VMEM), pl.BlockSpec(memory_space=pltpu.HBM)
    total = n * frames
    return pl.pallas_call(
        functools.partial(window_kernel, n),
        out_shape=jax.ShapeDtypeStruct((2 * frames, rows, cols, chan), BF16),
        in_specs=[hbm] * 11,
        out_specs=vmem,
        scratch_shapes=[
            pltpu.VMEM((frames, rows, cols, chan), BF16),
            pltpu.VMEM((frames + 2, rows, cols, 3 * chan), BF16),
            pltpu.VMEM((frames + 2, cols, chan), BF16),
            pltpu.VMEM((3, 3 * chan, 3 * chan), BF16),
            pltpu.VMEM((frames, rows, cols, 3 * chan), F32),
            pltpu.VMEM((frames, rows, cols, chan), BF16),
            pltpu.VMEM((chan, 3 * chan), BF16),
            pltpu.VMEM((chan, chan), BF16),
            pltpu.VMEM((3, chan, 2 * chan), BF16),
            pltpu.VMEM((total, per, chan), BF16),
            pltpu.VMEM((total * per, chan), BF16),
            pltpu.VMEM((total * per, chan), BF16),
            pltpu.VMEM((total + 2, per, chan), BF16),
            pltpu.VMEM((frames + 2, rows, cols, chan), BF16),
            pltpu.VMEM((chan,), BF16),
            pltpu.VMEM((chan,), BF16),
            pltpu.VMEM((chan,), BF16),
            pltpu.VMEM((2 * chan,), BF16),
            pltpu.SemaphoreType.DMA((10,)),
            pltpu.SemaphoreType.DMA((3, 9)),
            pltpu.SemaphoreType.DMA((3,)),
            pltpu.SemaphoreType.DMA((3,)),
            pltpu.SemaphoreType.DMA((2, n)),
            pltpu.SemaphoreType.DMA((2, n)),
            pltpu.SemaphoreType.DMA((n,)),
            pltpu.SemaphoreType.DMA((n,)),
        ],
        compiler_params=pltpu.CompilerParams(
            collective_id=0, has_side_effects=True, vmem_limit_bytes=56 * 1024 * 1024
        ),
    )(*args)


def solution(mesh):
    placed = (
        P(("groups", "tm"), "row", None, None),
        P(),
        P(),
        P(),
        P(),
        P(),
        P(),
        P(),
        P(),
        P(),
        P(),
    )
    return jax.shard_map(
        body,
        mesh=mesh,
        in_specs=placed,
        out_specs=P(("groups", "tm"), "row", None, None),
        check_vma=False,
    )
```

```python
import functools

import jax
import jax.numpy as jnp
from jax import lax
from jax.experimental import pallas as pl
from jax.experimental.pallas import tpu as pltpu
from jax.sharding import PartitionSpec as P


def shifted(value, axis, steps):
    count = lax.axis_size(axis)
    leading, last = (max(0, -steps), min(count, count - steps))
    return lax.ppermute(value, axis, [(source, source + steps) for source in range(leading, last)])


def with_halo(block, sides, width):
    for axis, dim in sides:
        count = lax.axis_size(axis)
        forward = [(i, i + 1) for i in range(count - 1)]
        backward = [(target, source) for source, target in forward]
        low = lax.ppermute(
            lax.slice_in_dim(block, block.shape[dim] - width, None, axis=dim), axis, forward
        )
        high = lax.ppermute(lax.slice_in_dim(block, 0, width, axis=dim), axis, backward)
        block = jnp.concatenate([low, block, high], axis=dim)
    return block


def channel_norm(values, gain):
    floats = values.astype(jnp.float32)
    return (
        floats
        * lax.rsqrt(jnp.mean(floats * floats, axis=-1, keepdims=True) + 1e-06)
        * gain.astype(jnp.float32)
    )


def attend(query, keys, values):
    frame_count = query.shape[0]
    channels = query.shape[2]
    scores = jnp.einsum(
        "tnc,snc->nts", query, keys, preferred_element_type=jnp.float32
    ) * channels ** (-0.5)
    later = lax.broadcasted_iota(jnp.int32, (frame_count, frame_count), 0)
    earlier = lax.broadcasted_iota(jnp.int32, (frame_count, frame_count), 1)
    causal_mask = (earlier <= later)[None]
    scores = jnp.where(causal_mask, scores, -1e30)
    highest = jnp.max(scores, axis=-1, keepdims=True)
    expo = jnp.where(causal_mask, jnp.exp(scores - highest), 0.0)
    weights = (expo / jnp.sum(expo, axis=-1, keepdims=True)).astype(jnp.bfloat16)
    return jnp.einsum("nts,snc->tnc", weights, values, preferred_element_type=jnp.float32).astype(
        jnp.bfloat16
    )


def flatten_block(block):
    return block.reshape(block.shape[0], block.shape[2], block.shape[3])


def plain_body(
    latent,
    conv_gain,
    conv_weight,
    conv_bias,
    attn_gain,
    w_query,
    w_key,
    w_value,
    w_out,
    time_weight,
    time_bias,
):
    frame_count, row_count, col_count, channels = latent.shape
    peers = lax.axis_size("tm")
    activated = jax.nn.silu(channel_norm(latent, conv_gain)).astype(jnp.bfloat16)
    carried = shifted(activated[frame_count - 2 :], "tm", 1)
    extended = jnp.concatenate([carried, activated], axis=0)
    padded = with_halo(extended, (("row", 1),), 1)
    padded = jnp.pad(padded, ((0, 0), (0, 0), (1, 1), (0, 0)))
    summed = jnp.zeros((frame_count * row_count * col_count, channels), jnp.float32)
    for offset in range(3):
        patches = jnp.concatenate(
            [
                padded[
                    offset : offset + frame_count,
                    row_offset : row_offset + row_count,
                    col_offset : col_offset + col_count,
                ]
                for row_offset in range(3)
                for col_offset in range(3)
            ],
            axis=-1,
        )
        summed = summed + jnp.dot(
            patches.reshape(-1, 9 * channels),
            conv_weight[offset].reshape(9 * channels, channels),
            preferred_element_type=jnp.float32,
        )
    hidden = (
        latent.astype(jnp.float32) + summed.reshape(latent.shape) + conv_bias.astype(jnp.float32)
    ).astype(jnp.bfloat16)
    attn_in = channel_norm(hidden, attn_gain).astype(jnp.bfloat16)
    positions = row_count * col_count
    per_peer = positions // peers
    blocked = attn_in.reshape(frame_count, peers, per_peer, channels)
    flat = flatten_block(lax.all_to_all(blocked, "tm", split_axis=1, concat_axis=0, tiled=True))
    stacked = flat.reshape(-1, channels)

    def project(matrix):
        return (
            jnp.dot(stacked, matrix, preferred_element_type=jnp.float32)
            .astype(jnp.bfloat16)
            .reshape(flat.shape)
        )

    attended = attend(project(w_query), project(w_key), project(w_value))[:, None]
    returned = lax.all_to_all(attended, "tm", split_axis=0, concat_axis=1, tiled=True)
    mixed_term = jnp.dot(
        returned.reshape(-1, channels), w_out, preferred_element_type=jnp.float32
    ).reshape(latent.shape)
    mixed = (hidden.astype(jnp.float32) + mixed_term).astype(jnp.bfloat16)
    mixed_cache = shifted(mixed[frame_count - 2 :], "tm", 1)
    mixed_ext = jnp.concatenate([mixed_cache, mixed], axis=0)
    doubled = jnp.zeros(
        (frame_count * row_count * col_count, 2 * channels), jnp.float32
    ) + time_bias.astype(jnp.float32)
    for offset in range(3):
        doubled = doubled + jnp.dot(
            mixed_ext[offset : offset + frame_count].reshape(-1, channels),
            time_weight[offset],
            preferred_element_type=jnp.float32,
        )
    doubled = doubled.reshape(frame_count, row_count, col_count, 2, channels).transpose(
        0, 3, 1, 2, 4
    )
    return doubled.reshape(2 * frame_count, row_count, col_count, channels).astype(jnp.bfloat16)


BF16, F32 = jnp.bfloat16, jnp.float32
MESH = pl.DeviceIdType.MESH


def unit(floats):
    return floats * lax.rsqrt(jnp.mean(floats * floats, axis=-1, keepdims=True) + 1e-06)


def dot(left, right):
    return jnp.dot(left, right, preferred_element_type=F32)


def window_kernel(
    n,
    latent_hbm,
    cgain_hbm,
    cw_hbm,
    cbias_hbm,
    again_hbm,
    wq_hbm,
    wk_hbm,
    wv_hbm,
    wo_hbm,
    tw_hbm,
    tbias_hbm,
    out,
    lat,
    lhs,
    rowh,
    cw,
    acc,
    hid,
    wqkv,
    wo,
    tw,
    x,
    kbuf,
    vbuf,
    mbuf,
    mext,
    cgain,
    cbias,
    again,
    tbias,
    load_sem,
    cw_sem,
    halo_send,
    halo_recv,
    a_send,
    a_recv,
    b_send,
    b_recv,
):
    frames, rows, cols, chan = lat.shape
    per = rows * cols // n
    own = frames * per
    me = lax.axis_index("tm")
    row = lax.axis_index("row")
    other = 1 - row

    loads = [pltpu.make_async_copy(latent_hbm, lat, load_sem.at[0])]
    for i, w in enumerate((wq_hbm, wk_hbm, wv_hbm)):
        loads.append(
            pltpu.make_async_copy(w, wqkv.at[:, pl.ds(i * chan, chan)], load_sem.at[1 + i])
        )
    loads.append(pltpu.make_async_copy(wo_hbm, wo, load_sem.at[4]))
    loads.append(pltpu.make_async_copy(again_hbm, again, load_sem.at[5]))
    loads.append(pltpu.make_async_copy(tbias_hbm, tbias, load_sem.at[6]))
    loads.append(pltpu.make_async_copy(tw_hbm, tw, load_sem.at[7]))
    gain_load = pltpu.make_async_copy(cgain_hbm, cgain, load_sem.at[8])
    bias_load = pltpu.make_async_copy(cbias_hbm, cbias, load_sem.at[9])
    cw_loads = {
        (a, b, e): pltpu.make_async_copy(
            cw_hbm.at[a, b, e],
            cw.at[a, pl.ds(b * chan, chan), pl.ds(e * chan, chan)],
            cw_sem.at[a, 3 * b + e],
        )
        for a in (2, 1, 0)
        for b in range(3)
        for e in range(3)
    }
    loads[0].start()
    gain_load.start()
    bias_load.start()
    barrier = pltpu.get_barrier_semaphore()
    for k in range(1, n):
        pl.semaphore_signal(
            barrier, inc=1, device_id={"tm": lax.rem(me + k, n)}, device_id_type=MESH
        )
    pl.semaphore_signal(barrier, inc=1, device_id={"row": other}, device_id_type=MESH)

    for c in cw_loads.values():
        c.start()
    for c in loads[1:]:
        c.start()

    loads[0].wait()
    gain_load.wait()
    bias_load.wait()
    gain = cgain[...].astype(F32).reshape(1, 1, 1, chan)
    normed = unit(lat[...].astype(F32)) * gain
    act = (normed / (1.0 + jnp.exp(-normed))).astype(BF16)
    mid = pl.ds(chan, chan)
    lhs[2:, :, :, chan : 2 * chan] = act

    pl.semaphore_wait(barrier, n)

    to_next = pltpu.make_async_remote_copy(
        lhs.at[pl.ds(frames, 2), :, :, mid],
        lhs.at[pl.ds(0, 2), :, :, mid],
        halo_send.at[0],
        halo_recv.at[0],
        device_id={"tm": jnp.minimum(me + 1, n - 1)},
        device_id_type=MESH,
    )
    to_row = pltpu.make_async_remote_copy(
        lhs.at[pl.ds(2, frames), other, :, mid],
        rowh.at[pl.ds(2, frames)],
        halo_send.at[1],
        halo_recv.at[1],
        device_id={"row": other},
        device_id_type=MESH,
    )
    relay = pltpu.make_async_remote_copy(
        lhs.at[pl.ds(0, 2), other, :, mid],
        rowh.at[pl.ds(0, 2)],
        halo_send.at[2],
        halo_recv.at[2],
        device_id={"row": other},
        device_id_type=MESH,
    )

    @pl.when(me < n - 1)
    def _():
        to_next.start()

    to_row.start()

    def spread(lo, hi):
        lhs[lo:hi, 1, :, 0:chan] = lhs[lo:hi, 0, :, chan : 2 * chan]
        lhs[lo:hi, 0, :, 2 * chan :] = lhs[lo:hi, 1, :, chan : 2 * chan]

    def edges(lo, hi):
        edge = rowh[lo:hi]
        lhs[lo:hi, 0, :, 0:chan] = jnp.where(row == 1, edge, jnp.zeros_like(edge))
        lhs[lo:hi, 1, :, 2 * chan :] = jnp.where(row == 0, edge, jnp.zeros_like(edge))

    spread(2, frames + 2)
    to_row.wait_recv()
    edges(2, frames + 2)

    def taps(lo, hi, a):
        part = lhs[lo:hi].reshape((hi - lo) * rows * cols, 3 * chan)
        return dot(part, cw[a]).reshape(hi - lo, rows, cols, 3 * chan)

    def loaded(a):
        for b in range(3):
            for e in range(3):
                cw_loads[a, b, e].wait()

    loaded(2)
    acc[...] = taps(2, frames + 2, 2)
    loaded(1)
    acc[1:] += taps(2, frames + 1, 1)
    loaded(0)
    acc[2:] += taps(2, frames, 0)

    bias = cbias[...].astype(F32).reshape(1, chan)

    def finish(lo, hi):
        m = (hi - lo) * rows * cols
        y = acc[lo:hi].reshape(m, 3 * chan)
        col = lax.rem(lax.broadcasted_iota(jnp.int32, (m, chan), 0), cols)
        left = jnp.where(col == 0, 0.0, pltpu.roll(y[:, :chan], 1, 0))
        right = jnp.where(col == cols - 1, 0.0, pltpu.roll(y[:, 2 * chan :], m - 1, 0))
        total = left + y[:, chan : 2 * chan] + right
        value = lat[lo:hi].astype(F32).reshape(m, chan) + total + bias
        hid[lo:hi] = value.astype(BF16).reshape(hi - lo, rows, cols, chan)

    def place(p):
        return p * per // cols, pl.ds(p * per % cols, per)

    def scatter_copies(half, p):
        lo, count = (2, frames - 2) if half == 0 else (0, 2)
        r, c = place(p)
        source = hid.at[pl.ds(lo, count), r, c]
        target = x.at[pl.ds(frames * me + lo, count)]
        remote = pltpu.make_async_remote_copy(
            source,
            target,
            a_send.at[half, p],
            a_recv.at[half, me],
            device_id={"tm": p},
            device_id_type=MESH,
        )
        local = pltpu.make_async_copy(source, target, a_recv.at[half, me])
        return remote, local

    def start_to(copies, p):
        remote, local = copies

        @pl.when(p != me)
        def _():
            remote.start()

        @pl.when(p == me)
        def _():
            local.start()

    def send_done(copies, p):
        remote = copies[0]

        @pl.when(p != me)
        def _():
            remote.wait_send()

    finish(2, frames)
    for p in range(n):
        start_to(scatter_copies(0, p), p)

    @pl.when(me > 0)
    def _():
        to_next.wait_recv()
        relay.start()

    @pl.when(me == 0)
    def _():
        lhs[0:2, :, :, chan : 2 * chan] = jnp.zeros((2, rows, cols, chan), BF16)
        rowh[0:2] = jnp.zeros((2, cols, chan), BF16)

    spread(0, 2)

    @pl.when(me > 0)
    def _():
        relay.wait_recv()

    edges(0, 2)
    acc[0:1] += taps(1, 2, 1)
    acc[0:2] += taps(0, 2, 0)
    finish(0, 2)
    for p in range(n):
        start_to(scatter_copies(1, p), p)

    for c in loads[1:]:
        c.wait()
    mbuf[0:2] = jnp.zeros((2, per, chan), BF16)
    gain2 = again[...].astype(F32).reshape(1, chan)

    def return_copies(p):
        r, c = place(0)
        first = me * per
        source = mbuf.at[pl.ds(frames * p, frames + 2)]
        target = mext.at[:, first // cols, pl.ds(pl.multiple_of(lax.rem(first, cols), per), per)]
        remote = pltpu.make_async_remote_copy(
            source,
            target,
            b_send.at[p],
            b_recv.at[me],
            device_id={"tm": p},
            device_id_type=MESH,
        )
        return remote, pltpu.make_async_copy(source, target, b_recv.at[me])

    group = 2 if n % 2 == 0 else 1
    m = group * own
    for j in range(n // group):
        for p in range(j * group, (j + 1) * group):
            for half, (lo, count) in enumerate(((2, frames - 2), (0, 2))):
                landed = x.at[pl.ds(frames * p + lo, count)]
                pltpu.make_async_copy(landed, landed, a_recv.at[half, p]).wait()
        block = x[j * group * frames : (j + 1) * group * frames].reshape(m, chan).astype(F32)
        qkv = dot((unit(block) * gain2).astype(BF16), wqkv[...]).astype(BF16)
        kbuf[j * m : (j + 1) * m] = qkv[:, chan : 2 * chan]
        vbuf[j * m : (j + 1) * m] = qkv[:, 2 * chan :]
        width = (j + 1) * m
        scores = lax.dot_general(
            qkv[:, :chan],
            kbuf[:width],
            (((1,), (1,)), ((), ())),
            preferred_element_type=F32,
        ) * chan ** (-0.5)
        query = lax.broadcasted_iota(jnp.int32, (m, width), 0) + j * m
        key = lax.broadcasted_iota(jnp.int32, (m, width), 1)
        seen = (lax.rem(query, per) == lax.rem(key, per)) & (key <= query)
        scores = jnp.where(seen, scores, -1e30)
        expo = jnp.where(seen, jnp.exp(scores - jnp.max(scores, axis=-1, keepdims=True)), 0.0)
        weights = (expo / jnp.sum(expo, axis=-1, keepdims=True)).astype(BF16)
        attended = dot(weights, vbuf[:width]).astype(BF16)
        mixed = (block + dot(attended, wo[...])).astype(BF16)
        mbuf[2 + j * group * frames : 2 + (j + 1) * group * frames] = mixed.reshape(
            group * frames, per, chan
        )
        for p in range(j * group, (j + 1) * group):
            start_to(return_copies(p), p)

    for p in range(n):
        r, c = place(p)
        landed = mext.at[:, r, c]
        pltpu.make_async_copy(landed, landed, b_recv.at[p]).wait()
    doubled = tbias[...].astype(F32).reshape(1, 2 * chan)
    for a in range(3):
        doubled = doubled + dot(mext[a : a + frames].reshape(-1, chan), tw[a])
    doubled = doubled.astype(BF16).reshape(frames, rows, cols, 2 * chan)
    for t in range(frames):
        out[2 * t] = doubled[t, :, :, :chan]
        out[2 * t + 1] = doubled[t, :, :, chan:]

    @pl.when(me < n - 1)
    def _():
        to_next.wait_send()

    to_row.wait_send()

    @pl.when(me > 0)
    def _():
        relay.wait_send()

    for p in range(n):
        send_done(scatter_copies(0, p), p)
        send_done(scatter_copies(1, p), p)
        send_done(return_copies(p), p)


def body(*args):
    latent = args[0]
    frames, rows, cols, chan = latent.shape
    n = lax.axis_size("tm")
    per = rows * cols // n
    tiled = per and per % 16 == 0 and cols % per == 0 and frames > 2
    if not tiled or lax.axis_size("row") != 2:
        return plain_body(*args)
    vmem, hbm = pl.BlockSpec(memory_space=pltpu.VMEM), pl.BlockSpec(memory_space=pltpu.HBM)
    total = n * frames
    return pl.pallas_call(
        functools.partial(window_kernel, n),
        out_shape=jax.ShapeDtypeStruct((2 * frames, rows, cols, chan), BF16),
        in_specs=[hbm] * 11,
        out_specs=vmem,
        scratch_shapes=[
            pltpu.VMEM((frames, rows, cols, chan), BF16),
            pltpu.VMEM((frames + 2, rows, cols, 3 * chan), BF16),
            pltpu.VMEM((frames + 2, cols, chan), BF16),
            pltpu.VMEM((3, 3 * chan, 3 * chan), BF16),
            pltpu.VMEM((frames, rows, cols, 3 * chan), F32),
            pltpu.VMEM((frames, rows, cols, chan), BF16),
            pltpu.VMEM((chan, 3 * chan), BF16),
            pltpu.VMEM((chan, chan), BF16),
            pltpu.VMEM((3, chan, 2 * chan), BF16),
            pltpu.VMEM((total, per, chan), BF16),
            pltpu.VMEM((total * per, chan), BF16),
            pltpu.VMEM((total * per, chan), BF16),
            pltpu.VMEM((total + 2, per, chan), BF16),
            pltpu.VMEM((frames + 2, rows, cols, chan), BF16),
            pltpu.VMEM((chan,), BF16),
            pltpu.VMEM((chan,), BF16),
            pltpu.VMEM((chan,), BF16),
            pltpu.VMEM((2 * chan,), BF16),
            pltpu.SemaphoreType.DMA((10,)),
            pltpu.SemaphoreType.DMA((3, 9)),
            pltpu.SemaphoreType.DMA((3,)),
            pltpu.SemaphoreType.DMA((3,)),
            pltpu.SemaphoreType.DMA((2, n)),
            pltpu.SemaphoreType.DMA((2, n)),
            pltpu.SemaphoreType.DMA((n,)),
            pltpu.SemaphoreType.DMA((n,)),
        ],
        compiler_params=pltpu.CompilerParams(
            collective_id=0, has_side_effects=True, vmem_limit_bytes=56 * 1024 * 1024
        ),
    )(*args)


def solution(mesh):
    placed = (
        P(("groups", "tm"), "row", None, None),
        P(),
        P(),
        P(),
        P(),
        P(),
        P(),
        P(),
        P(),
        P(),
        P(),
    )
    return jax.shard_map(
        body,
        mesh=mesh,
        in_specs=placed,
        out_specs=P(("groups", "tm"), "row", None, None),
        check_vma=False,
    )
```

```python
import functools

import jax
import jax.numpy as jnp
from jax import lax
from jax.experimental import pallas as pl
from jax.experimental.pallas import tpu as pltpu
from jax.sharding import PartitionSpec as P


def shifted(value, axis, steps):
    count = lax.axis_size(axis)
    leading, last = (max(0, -steps), min(count, count - steps))
    return lax.ppermute(value, axis, [(source, source + steps) for source in range(leading, last)])


def with_halo(block, sides, width):
    for axis, dim in sides:
        count = lax.axis_size(axis)
        forward = [(i, i + 1) for i in range(count - 1)]
        backward = [(target, source) for source, target in forward]
        low = lax.ppermute(
            lax.slice_in_dim(block, block.shape[dim] - width, None, axis=dim), axis, forward
        )
        high = lax.ppermute(lax.slice_in_dim(block, 0, width, axis=dim), axis, backward)
        block = jnp.concatenate([low, block, high], axis=dim)
    return block


def channel_norm(values, gain):
    floats = values.astype(jnp.float32)
    return (
        floats
        * lax.rsqrt(jnp.mean(floats * floats, axis=-1, keepdims=True) + 1e-06)
        * gain.astype(jnp.float32)
    )


def attend(query, keys, values):
    frame_count = query.shape[0]
    channels = query.shape[2]
    scores = jnp.einsum(
        "tnc,snc->nts", query, keys, preferred_element_type=jnp.float32
    ) * channels ** (-0.5)
    later = lax.broadcasted_iota(jnp.int32, (frame_count, frame_count), 0)
    earlier = lax.broadcasted_iota(jnp.int32, (frame_count, frame_count), 1)
    causal_mask = (earlier <= later)[None]
    scores = jnp.where(causal_mask, scores, -1e30)
    highest = jnp.max(scores, axis=-1, keepdims=True)
    expo = jnp.where(causal_mask, jnp.exp(scores - highest), 0.0)
    weights = (expo / jnp.sum(expo, axis=-1, keepdims=True)).astype(jnp.bfloat16)
    return jnp.einsum("nts,snc->tnc", weights, values, preferred_element_type=jnp.float32).astype(
        jnp.bfloat16
    )


def flatten_block(block):
    return block.reshape(block.shape[0], block.shape[2], block.shape[3])


def plain_body(
    latent,
    conv_gain,
    conv_weight,
    conv_bias,
    attn_gain,
    w_query,
    w_key,
    w_value,
    w_out,
    time_weight,
    time_bias,
):
    frame_count, row_count, col_count, channels = latent.shape
    peers = lax.axis_size("tm")
    activated = jax.nn.silu(channel_norm(latent, conv_gain)).astype(jnp.bfloat16)
    carried = shifted(activated[frame_count - 2 :], "tm", 1)
    extended = jnp.concatenate([carried, activated], axis=0)
    padded = with_halo(extended, (("row", 1),), 1)
    padded = jnp.pad(padded, ((0, 0), (0, 0), (1, 1), (0, 0)))
    summed = jnp.zeros((frame_count * row_count * col_count, channels), jnp.float32)
    for offset in range(3):
        patches = jnp.concatenate(
            [
                padded[
                    offset : offset + frame_count,
                    row_offset : row_offset + row_count,
                    col_offset : col_offset + col_count,
                ]
                for row_offset in range(3)
                for col_offset in range(3)
            ],
            axis=-1,
        )
        summed = summed + jnp.dot(
            patches.reshape(-1, 9 * channels),
            conv_weight[offset].reshape(9 * channels, channels),
            preferred_element_type=jnp.float32,
        )
    hidden = (
        latent.astype(jnp.float32) + summed.reshape(latent.shape) + conv_bias.astype(jnp.float32)
    ).astype(jnp.bfloat16)
    attn_in = channel_norm(hidden, attn_gain).astype(jnp.bfloat16)
    positions = row_count * col_count
    per_peer = positions // peers
    blocked = attn_in.reshape(frame_count, peers, per_peer, channels)
    flat = flatten_block(lax.all_to_all(blocked, "tm", split_axis=1, concat_axis=0, tiled=True))
    stacked = flat.reshape(-1, channels)

    def project(matrix):
        return (
            jnp.dot(stacked, matrix, preferred_element_type=jnp.float32)
            .astype(jnp.bfloat16)
            .reshape(flat.shape)
        )

    attended = attend(project(w_query), project(w_key), project(w_value))[:, None]
    returned = lax.all_to_all(attended, "tm", split_axis=0, concat_axis=1, tiled=True)
    mixed_term = jnp.dot(
        returned.reshape(-1, channels), w_out, preferred_element_type=jnp.float32
    ).reshape(latent.shape)
    mixed = (hidden.astype(jnp.float32) + mixed_term).astype(jnp.bfloat16)
    mixed_cache = shifted(mixed[frame_count - 2 :], "tm", 1)
    mixed_ext = jnp.concatenate([mixed_cache, mixed], axis=0)
    doubled = jnp.zeros(
        (frame_count * row_count * col_count, 2 * channels), jnp.float32
    ) + time_bias.astype(jnp.float32)
    for offset in range(3):
        doubled = doubled + jnp.dot(
            mixed_ext[offset : offset + frame_count].reshape(-1, channels),
            time_weight[offset],
            preferred_element_type=jnp.float32,
        )
    doubled = doubled.reshape(frame_count, row_count, col_count, 2, channels).transpose(
        0, 3, 1, 2, 4
    )
    return doubled.reshape(2 * frame_count, row_count, col_count, channels).astype(jnp.bfloat16)


BF16, F32 = jnp.bfloat16, jnp.float32
MESH = pl.DeviceIdType.MESH


def unit(floats):
    return floats * lax.rsqrt(jnp.mean(floats * floats, axis=-1, keepdims=True) + 1e-06)


def dot(left, right):
    return jnp.dot(left, right, preferred_element_type=F32)


def window_kernel(
    n,
    latent_hbm,
    cgain_hbm,
    cw_hbm,
    cbias_hbm,
    again_hbm,
    wq_hbm,
    wk_hbm,
    wv_hbm,
    wo_hbm,
    tw_hbm,
    tbias_hbm,
    out,
    lat,
    lhs,
    rowh,
    cw,
    acc,
    hid,
    wqkv,
    wo,
    tw,
    x,
    kbuf,
    vbuf,
    mbuf,
    mext,
    cgain,
    cbias,
    again,
    tbias,
    load_sem,
    cw_sem,
    halo_send,
    halo_recv,
    a_send,
    a_recv,
    b_send,
    b_recv,
):
    frames, rows, cols, chan = lat.shape
    per = rows * cols // n
    own = frames * per
    me = lax.axis_index("tm")
    row = lax.axis_index("row")
    other = 1 - row

    loads = [pltpu.make_async_copy(latent_hbm, lat, load_sem.at[0])]
    for i, w in enumerate((wq_hbm, wk_hbm, wv_hbm)):
        loads.append(
            pltpu.make_async_copy(w, wqkv.at[:, pl.ds(i * chan, chan)], load_sem.at[1 + i])
        )
    loads.append(pltpu.make_async_copy(wo_hbm, wo, load_sem.at[4]))
    loads.append(pltpu.make_async_copy(again_hbm, again, load_sem.at[5]))
    loads.append(pltpu.make_async_copy(tbias_hbm, tbias, load_sem.at[6]))
    loads.append(pltpu.make_async_copy(tw_hbm, tw, load_sem.at[7]))
    gain_load = pltpu.make_async_copy(cgain_hbm, cgain, load_sem.at[8])
    bias_load = pltpu.make_async_copy(cbias_hbm, cbias, load_sem.at[9])
    cw_loads = {
        (a, b, e): pltpu.make_async_copy(
            cw_hbm.at[a, b, e],
            cw.at[a, pl.ds(b * chan, chan), pl.ds(e * chan, chan)],
            cw_sem.at[a, 3 * b + e],
        )
        for a in (2, 1, 0)
        for b in range(3)
        for e in range(3)
    }
    loads[0].start()
    gain_load.start()
    bias_load.start()
    barrier = pltpu.get_barrier_semaphore()
    for k in range(1, n):
        pl.semaphore_signal(
            barrier, inc=1, device_id={"tm": lax.rem(me + k, n)}, device_id_type=MESH
        )
    pl.semaphore_signal(barrier, inc=1, device_id={"row": other}, device_id_type=MESH)

    for c in cw_loads.values():
        c.start()

    loads[0].wait()
    gain_load.wait()
    bias_load.wait()
    gain = cgain[...].astype(F32).reshape(1, 1, 1, chan)
    normed = unit(lat[...].astype(F32)) * gain
    act = (normed / (1.0 + jnp.exp(-normed))).astype(BF16)
    mid = pl.ds(chan, chan)
    lhs[2:, :, :, chan : 2 * chan] = act

    pl.semaphore_wait(barrier, n)

    to_next = pltpu.make_async_remote_copy(
        lhs.at[pl.ds(frames, 2), :, :, mid],
        lhs.at[pl.ds(0, 2), :, :, mid],
        halo_send.at[0],
        halo_recv.at[0],
        device_id={"tm": jnp.minimum(me + 1, n - 1)},
        device_id_type=MESH,
    )
    to_row = pltpu.make_async_remote_copy(
        lhs.at[pl.ds(2, frames), other, :, mid],
        rowh.at[pl.ds(2, frames)],
        halo_send.at[1],
        halo_recv.at[1],
        device_id={"row": other},
        device_id_type=MESH,
    )
    relay = pltpu.make_async_remote_copy(
        lhs.at[pl.ds(0, 2), other, :, mid],
        rowh.at[pl.ds(0, 2)],
        halo_send.at[2],
        halo_recv.at[2],
        device_id={"row": other},
        device_id_type=MESH,
    )

    @pl.when(me < n - 1)
    def _():
        to_next.start()

    to_row.start()
    for c in loads[1:]:
        c.start()

    def spread(lo, hi):
        lhs[lo:hi, 1, :, 0:chan] = lhs[lo:hi, 0, :, chan : 2 * chan]
        lhs[lo:hi, 0, :, 2 * chan :] = lhs[lo:hi, 1, :, chan : 2 * chan]

    def edges(lo, hi):
        edge = rowh[lo:hi]
        lhs[lo:hi, 0, :, 0:chan] = jnp.where(row == 1, edge, jnp.zeros_like(edge))
        lhs[lo:hi, 1, :, 2 * chan :] = jnp.where(row == 0, edge, jnp.zeros_like(edge))

    spread(2, frames + 2)
    to_row.wait_recv()
    edges(2, frames + 2)

    def taps(lo, hi, a):
        part = lhs[lo:hi].reshape((hi - lo) * rows * cols, 3 * chan)
        return dot(part, cw[a]).reshape(hi - lo, rows, cols, 3 * chan)

    def loaded(a):
        for b in range(3):
            for e in range(3):
                cw_loads[a, b, e].wait()

    loaded(2)
    acc[...] = taps(2, frames + 2, 2)
    loaded(1)
    acc[1:] += taps(2, frames + 1, 1)
    loaded(0)
    acc[2:] += taps(2, frames, 0)

    bias = cbias[...].astype(F32).reshape(1, chan)

    def finish(lo, hi):
        m = (hi - lo) * rows * cols
        y = acc[lo:hi].reshape(m, 3 * chan)
        col = lax.rem(lax.broadcasted_iota(jnp.int32, (m, chan), 0), cols)
        left = jnp.where(col == 0, 0.0, pltpu.roll(y[:, :chan], 1, 0))
        right = jnp.where(col == cols - 1, 0.0, pltpu.roll(y[:, 2 * chan :], m - 1, 0))
        total = left + y[:, chan : 2 * chan] + right
        value = lat[lo:hi].astype(F32).reshape(m, chan) + total + bias
        hid[lo:hi] = value.astype(BF16).reshape(hi - lo, rows, cols, chan)

    def place(p):
        return p * per // cols, pl.ds(p * per % cols, per)

    def scatter_copies(half, p):
        lo, count = (2, frames - 2) if half == 0 else (0, 2)
        r, c = place(p)
        source = hid.at[pl.ds(lo, count), r, c]
        target = x.at[pl.ds(frames * me + lo, count)]
        remote = pltpu.make_async_remote_copy(
            source,
            target,
            a_send.at[half, p],
            a_recv.at[half, me],
            device_id={"tm": p},
            device_id_type=MESH,
        )
        local = pltpu.make_async_copy(source, target, a_recv.at[half, me])
        return remote, local

    def start_to(copies, p):
        remote, local = copies

        @pl.when(p != me)
        def _():
            remote.start()

        @pl.when(p == me)
        def _():
            local.start()

    def send_done(copies, p):
        remote = copies[0]

        @pl.when(p != me)
        def _():
            remote.wait_send()

    finish(2, frames)
    for p in range(n):
        start_to(scatter_copies(0, p), p)

    @pl.when(me > 0)
    def _():
        to_next.wait_recv()
        relay.start()

    @pl.when(me == 0)
    def _():
        lhs[0:2, :, :, chan : 2 * chan] = jnp.zeros((2, rows, cols, chan), BF16)
        rowh[0:2] = jnp.zeros((2, cols, chan), BF16)

    spread(0, 2)

    @pl.when(me > 0)
    def _():
        relay.wait_recv()

    edges(0, 2)
    acc[0:1] += taps(1, 2, 1)
    acc[0:2] += taps(0, 2, 0)
    finish(0, 2)
    for p in range(n):
        start_to(scatter_copies(1, p), p)

    for c in loads[1:]:
        c.wait()
    mbuf[0:2] = jnp.zeros((2, per, chan), BF16)
    gain2 = again[...].astype(F32).reshape(1, chan)

    def return_copies(p):
        r, c = place(0)
        first = me * per
        source = mbuf.at[pl.ds(frames * p, frames + 2)]
        target = mext.at[:, first // cols, pl.ds(pl.multiple_of(lax.rem(first, cols), per), per)]
        remote = pltpu.make_async_remote_copy(
            source,
            target,
            b_send.at[p],
            b_recv.at[me],
            device_id={"tm": p},
            device_id_type=MESH,
        )
        return remote, pltpu.make_async_copy(source, target, b_recv.at[me])

    group = 2 if n % 2 == 0 else 1
    m = group * own
    for j in range(n // group):
        for p in range(j * group, (j + 1) * group):
            for half, (lo, count) in enumerate(((2, frames - 2), (0, 2))):
                landed = x.at[pl.ds(frames * p + lo, count)]
                pltpu.make_async_copy(landed, landed, a_recv.at[half, p]).wait()
        block = x[j * group * frames : (j + 1) * group * frames].reshape(m, chan).astype(F32)
        qkv = dot((unit(block) * gain2).astype(BF16), wqkv[...]).astype(BF16)
        kbuf[j * m : (j + 1) * m] = qkv[:, chan : 2 * chan]
        vbuf[j * m : (j + 1) * m] = qkv[:, 2 * chan :]
        width = (j + 1) * m
        scores = lax.dot_general(
            qkv[:, :chan],
            kbuf[:width],
            (((1,), (1,)), ((), ())),
            preferred_element_type=F32,
        ) * chan ** (-0.5)
        query = lax.broadcasted_iota(jnp.int32, (m, width), 0) + j * m
        key = lax.broadcasted_iota(jnp.int32, (m, width), 1)
        seen = (lax.rem(query, per) == lax.rem(key, per)) & (key <= query)
        scores = jnp.where(seen, scores, -1e30)
        expo = jnp.where(seen, jnp.exp(scores - jnp.max(scores, axis=-1, keepdims=True)), 0.0)
        weights = (expo / jnp.sum(expo, axis=-1, keepdims=True)).astype(BF16)
        attended = dot(weights, vbuf[:width]).astype(BF16)
        mixed = (block + dot(attended, wo[...])).astype(BF16)
        mbuf[2 + j * group * frames : 2 + (j + 1) * group * frames] = mixed.reshape(
            group * frames, per, chan
        )
        for p in range(j * group, (j + 1) * group):
            start_to(return_copies(p), p)

    for p in range(n):
        r, c = place(p)
        landed = mext.at[:, r, c]
        pltpu.make_async_copy(landed, landed, b_recv.at[p]).wait()
    doubled = tbias[...].astype(F32).reshape(1, 2 * chan)
    for a in range(3):
        doubled = doubled + dot(mext[a : a + frames].reshape(-1, chan), tw[a])
    doubled = doubled.astype(BF16).reshape(frames, rows, cols, 2 * chan)
    for t in range(frames):
        out[2 * t] = doubled[t, :, :, :chan]
        out[2 * t + 1] = doubled[t, :, :, chan:]

    @pl.when(me < n - 1)
    def _():
        to_next.wait_send()

    to_row.wait_send()

    @pl.when(me > 0)
    def _():
        relay.wait_send()

    for p in range(n):
        send_done(scatter_copies(0, p), p)
        send_done(scatter_copies(1, p), p)
        send_done(return_copies(p), p)


def body(*args):
    latent = args[0]
    frames, rows, cols, chan = latent.shape
    n = lax.axis_size("tm")
    per = rows * cols // n
    tiled = per and per % 16 == 0 and cols % per == 0 and frames > 2
    if not tiled or lax.axis_size("row") != 2:
        return plain_body(*args)
    vmem, hbm = pl.BlockSpec(memory_space=pltpu.VMEM), pl.BlockSpec(memory_space=pltpu.HBM)
    total = n * frames
    return pl.pallas_call(
        functools.partial(window_kernel, n),
        out_shape=jax.ShapeDtypeStruct((2 * frames, rows, cols, chan), BF16),
        in_specs=[hbm] * 11,
        out_specs=vmem,
        scratch_shapes=[
            pltpu.VMEM((frames, rows, cols, chan), BF16),
            pltpu.VMEM((frames + 2, rows, cols, 3 * chan), BF16),
            pltpu.VMEM((frames + 2, cols, chan), BF16),
            pltpu.VMEM((3, 3 * chan, 3 * chan), BF16),
            pltpu.VMEM((frames, rows, cols, 3 * chan), F32),
            pltpu.VMEM((frames, rows, cols, chan), BF16),
            pltpu.VMEM((chan, 3 * chan), BF16),
            pltpu.VMEM((chan, chan), BF16),
            pltpu.VMEM((3, chan, 2 * chan), BF16),
            pltpu.VMEM((total, per, chan), BF16),
            pltpu.VMEM((total * per, chan), BF16),
            pltpu.VMEM((total * per, chan), BF16),
            pltpu.VMEM((total + 2, per, chan), BF16),
            pltpu.VMEM((frames + 2, rows, cols, chan), BF16),
            pltpu.VMEM((chan,), BF16),
            pltpu.VMEM((chan,), BF16),
            pltpu.VMEM((chan,), BF16),
            pltpu.VMEM((2 * chan,), BF16),
            pltpu.SemaphoreType.DMA((10,)),
            pltpu.SemaphoreType.DMA((3, 9)),
            pltpu.SemaphoreType.DMA((3,)),
            pltpu.SemaphoreType.DMA((3,)),
            pltpu.SemaphoreType.DMA((2, n)),
            pltpu.SemaphoreType.DMA((2, n)),
            pltpu.SemaphoreType.DMA((n,)),
            pltpu.SemaphoreType.DMA((n,)),
        ],
        compiler_params=pltpu.CompilerParams(
            collective_id=0, has_side_effects=True, vmem_limit_bytes=56 * 1024 * 1024
        ),
    )(*args)


def solution(mesh):
    placed = (
        P(("groups", "tm"), "row", None, None),
        P(),
        P(),
        P(),
        P(),
        P(),
        P(),
        P(),
        P(),
        P(),
        P(),
    )
    return jax.shard_map(
        body,
        mesh=mesh,
        in_specs=placed,
        out_specs=P(("groups", "tm"), "row", None, None),
        check_vma=False,
    )
```
